256 devices in a mesh: dp: 32 (over y, x, core), mp: 8 (over z).
Axes of the slice: x: 4, y: 4, z: 8, core: 2. Of those that a mesh axis runs over, the one named last changes fastest.
Arguments:
- grads: bfloat16 [32, 1024, 1024], P('dp', None, 'mp')
- momentum: float32 [32, 1024, 1024], P('dp', None, 'mp'), may hold values from -6 to 6
- second_moment: float32 [32, 1024, 1024], P('dp', None, 'mp'), may hold values from 0.0001 to 0.01
- owners: int32 [32], replicated, may hold values from 0 to 31, as said below
- left_stats: float32 [32, 3, 1024, 1024], P('dp', None, 'mp'), may hold values from -6 to 6
- right_stats: float32 [32, 3, 1024, 1024], P('dp', None, 'mp'), may hold values from -6 to 6
- left_roots: bfloat16 [32, 3, 1024, 1024], P('dp', None, None, 'mp'), as said below
- right_roots: bfloat16 [32, 3, 1024, 1024], P('dp', None, None, 'mp'), as said below
Outputs:
- step: bfloat16 [32, 1024, 1024], P('dp', None, 'mp')
- momentum_out: float32 [32, 1024, 1024], P('dp', None, 'mp')
- left_out: float32 [32, 3, 1024, 1024], P('dp', None, 'mp')
- right_out: float32 [32, 3, 1024, 1024], P('dp', None, 'mp')
The draws below stay inside these ranges and needn't reach their ends.
Inputs may be any that keep to these rules, and one draw needn't show every extreme that they name: `owners`: each owner index appears at most 3 times, and one appears exactly 3 times. `left_roots`: each 1024 x 1024 block is symmetric. `right_roots`: each 1024 x 1024 block is symmetric.
All inputs are finite; a program needn't handle non-finite values.
Results may differ from the reference program's by a relative error of at most 0.0022.
Values may be sent and summed in bfloat16 or wider, within the bound.
A program may use at most 128 MiB of HBM per device.

```python
import math
import jax
import jax.numpy as jnp
from jax import lax

BS = 1024
NBLK = 32
SLOTS = 3
N_DP = 32


def log_uniform(key, shape, low, high):
    return jnp.exp(jax.random.uniform(key, shape, jnp.float32, math.log(low), math.log(high)))


def symmetric_root(raw_noise, diagonal):
    symmetric = (raw_noise + jnp.swapaxes(raw_noise, -1, -2)) * 0.5
    return symmetric * (0.5 / math.sqrt(BS)) + jnp.eye(BS, dtype=jnp.float32) * diagonal[..., :, None]


def draw_owners(key, part):
    key = jax.random.fold_in(key, 11)
    key_busy, key_pick, key_order = jax.random.split(key, 3)
    busiest = jax.random.randint(key_busy, (), 0, N_DP, dtype=jnp.int32)
    others = jnp.arange(N_DP - 1, dtype=jnp.int32)
    others = others + (others >= busiest).astype(jnp.int32)
    candidates = jnp.repeat(others, SLOTS)
    chosen = jax.random.permutation(key_pick, candidates)[:NBLK - SLOTS]
    listed = jnp.concatenate([jnp.full((SLOTS,), busiest, jnp.int32), chosen])
    return jax.random.permutation(key_order, listed).astype(jnp.int32)


def draw_grads(key, part):
    key = jax.random.fold_in(key, 31)
    key_base, key_rows, key_cols = jax.random.split(key, 3)
    base_values = jax.random.normal(key_base, (NBLK, BS, BS), jnp.float32)
    row_scale = log_uniform(key_rows, (NBLK, BS, 1), 0.01, 0.1)
    col_scale = log_uniform(key_cols, (NBLK, 1, BS), 0.3, 3.0)
    return (base_values * row_scale * col_scale).astype(jnp.bfloat16)


def draw_left_roots(key, part):
    key = jax.random.fold_in(key, 21)
    key_diag, key_off = jax.random.split(key)
    raw_noise = jax.random.normal(key_off, (N_DP, SLOTS, BS, BS), jnp.float32)
    diagonal = log_uniform(key_diag, (N_DP, SLOTS, BS), 0.5, 2.0)
    return symmetric_root(raw_noise, diagonal).astype(jnp.bfloat16)


def draw_right_roots(key, part):
    key = jax.random.fold_in(key, 22)
    key_diag, key_off = jax.random.split(key)
    raw_noise = jax.random.normal(key_off, (N_DP, SLOTS, BS, BS), jnp.float32)
    diagonal = log_uniform(key_diag, (N_DP, SLOTS, BS), 0.5, 2.0)
    return symmetric_root(raw_noise, diagonal).astype(jnp.bfloat16)


def block_levels(rng, shape, pieces, smallest, largest):
    level, own = 1.0, jax.random.fold_in(rng, 6)
    for axis_at, shards_of in pieces:
        steps = jnp.exp(jax.random.uniform(jax.random.fold_in(own, axis_at), (shards_of,), jnp.float32, smallest / len(pieces), largest / len(pieces)))
        level = level * jnp.repeat(steps, shape[axis_at] // shards_of).reshape([-1 if axis == axis_at else 1 for axis in range(len(shape))])
    return level


def noise(own_key, extent, spread, limit, shards=(), kind=jnp.bfloat16):
    values = spread * jax.random.normal(own_key, extent, jnp.float32)
    if shards:
        values = values * block_levels(own_key, extent, shards, -0.22, 0.18)
    return jnp.clip(values, -limit, limit).astype(kind)


def setup_inputs(seed: int = 0) -> dict:
    arg_keys = jax.random.split(jax.random.key(seed), 9)
    grads = draw_grads(jax.random.fold_in(arg_keys[8], 71), 0)
    momentum = noise(arg_keys[1], (NBLK, BS, BS), 1.0, 6.0, ((0, 32), (2, 8)), jnp.float32)
    second_moment = jnp.clip(jnp.exp(math.log(0.01) - 4.6051702 * jax.random.uniform(arg_keys[2], (NBLK, BS, BS), jnp.float32) ** block_levels(arg_keys[2], (NBLK, BS, BS), ((0, 32), (2, 8)), -0.2, 0.2)), 0.0001, 0.01)
    owners = draw_owners(jax.random.fold_in(arg_keys[8], 71), 0)
    left_stats = noise(arg_keys[4], (N_DP, SLOTS, BS, BS), 1.0, 6.0, ((0, 32), (2, 8)), jnp.float32)
    right_stats = noise(arg_keys[5], (N_DP, SLOTS, BS, BS), 1.0, 6.0, ((0, 32), (2, 8)), jnp.float32)
    left_roots = draw_left_roots(jax.random.fold_in(arg_keys[8], 71), 0)
    right_roots = draw_right_roots(jax.random.fold_in(arg_keys[8], 71), 0)
    return dict(grads=grads, momentum=momentum, second_moment=second_moment, owners=owners, left_stats=left_stats, right_stats=right_stats, left_roots=left_roots, right_roots=right_roots)


beta_one = 0.9
beta_adam = 0.99
beta_stat = 0.95
adam_eps = 1e-08
norm_eps = 1e-06
step_rate = 0.5

def slot_table(owners):
    positions = jnp.arange(owners.shape[0], dtype=jnp.int32)
    same_owner = owners[:, None] == owners[None, :]
    earlier = positions[None, :] < positions[:, None]
    return lax.optimization_barrier(jnp.sum((same_owner & earlier).astype(jnp.int32), axis=1)).astype(jnp.int32)

def reference(grads, momentum, second_moment, owners, left_stats, right_stats, left_roots, right_roots):
    grad_wide = grads.astype(jnp.float32)
    second_new = beta_adam * second_moment + (1.0 - beta_adam) * grad_wide * grad_wide
    adam_dir = grad_wide / (jnp.sqrt(second_new) + adam_eps)
    adam_sq = lax.optimization_barrier(jnp.sum(adam_dir * adam_dir, axis=(1, 2))).astype(jnp.bfloat16)
    slot_of = slot_table(owners)

    def one_block(block_index):
        gradient = grads[block_index]
        owner_now = owners[block_index]
        slot_now = slot_of[block_index]
        left_root = left_roots[owner_now, slot_now]
        right_root = right_roots[owner_now, slot_now]
        left_gram = jnp.dot(gradient, gradient.T, preferred_element_type=jnp.float32)
        right_gram = jnp.dot(gradient.T, gradient, preferred_element_type=jnp.float32)
        mixed = jnp.dot(gradient, right_root, preferred_element_type=jnp.float32).astype(jnp.bfloat16)
        precond = jnp.dot(left_root, mixed, preferred_element_type=jnp.float32)
        precond_sq = jnp.sum(precond * precond)
        graft_scale = jnp.sqrt(adam_sq[block_index].astype(jnp.float32) / (precond_sq + norm_eps))
        return ((precond * graft_scale).astype(jnp.bfloat16), left_gram, right_gram)
    graft_dir, left_gram, right_gram = lax.map(one_block, jnp.arange(NBLK, dtype=jnp.int32))
    zero_stats = jnp.zeros(left_stats.shape, jnp.float32)
    left_out = beta_stat * left_stats + (1.0 - beta_stat) * zero_stats.at[owners, slot_of].set(left_gram)
    right_out = beta_stat * right_stats + (1.0 - beta_stat) * zero_stats.at[owners, slot_of].set(right_gram)
    momentum_out = beta_one * momentum + (1.0 - beta_one) * graft_dir.astype(jnp.float32)
    step = (-step_rate * momentum_out).astype(jnp.bfloat16)
    return (step, momentum_out, left_out, right_out)
```

```python
import jax
import jax.numpy as jnp
from jax import lax
from jax.experimental import pallas as pl
from jax.experimental.pallas import tpu as pltpu
from jax.sharding import PartitionSpec as P

beta_one = 0.9
beta_adam = 0.99
beta_stat = 0.95
adam_eps = 1e-08
norm_eps = 1e-06
step_rate = 0.5

MESH = pl.DeviceIdType.MESH
NZ = 8
NG = 8
NT = 4
NS = 3
TILE = 128
BS = 1024
HALF = 5 * TILE
PIECE = HALF // NG
CH = 4
F32 = jnp.float32
BF16 = jnp.bfloat16


def dot(a, b, ca=1, cb=0):
    return lax.dot_general(a, b, (((ca,), (cb,)), ((), ())), preferred_element_type=F32)


def kernel(
    tbl, grads, second, left_roots, right_roots,
    graft, gram_l, gram_r,
    gbuf, sec, l_rot,
    a_r, a_l, t_r, t_l, b_r, b_l, c_r, c_l, d_r, d_l,
    l_all, rg, lg, f_r, f_l, h_r, h_l, acc, mext, gt, pre, ps,
    local_sem, zg_s, zg_r, zl_s, zl_r, ps_s, ps_r, s1_s, s1_r, s2_s, s2_r, s3_s, s3_r, g1_s, g1_r, g2_s, g2_r, g3_s, g3_r,
):
    d = lax.axis_index("dp")
    z = lax.axis_index("mp")
    core = d % 2
    x = (d // 2) % 4
    y = d // 8

    g_of = (x * 2 + core, y * 2 + core)
    t_of = (y, x)

    def dev(mode, g, t):
        if mode == 0:
            return t * 8 + g
        return (g // 2) * 8 + t * 2 + g % 2

    def group(mode, k):
        g = (g_of[mode] + k) % NG
        return g, dev(mode, g, t_of[mode])

    def other(mode, k):
        t = (t_of[mode] + k) % NT
        return t, dev(mode, g_of[mode], t)

    def remote(src, dst, ss, rs, to, zto):
        return pltpu.make_async_remote_copy(
            src_ref=src, dst_ref=dst, send_sem=ss, recv_sem=rs, device_id=(to, zto), device_id_type=MESH
        )

    sent = []

    def start(copy):
        copy.start()
        sent.append(copy)
        return copy

    own_g = pltpu.make_async_copy(grads.at[0], gbuf.at[z], local_sem.at[0])
    own_g.start()
    rot = []
    for j in range(5):
        row = pl.multiple_of(((z + j) % NZ) * TILE, TILE)
        copy = pltpu.make_async_copy(
            left_roots.at[0, :, pl.ds(row, TILE), :], l_rot.at[:, pl.ds(j * TILE, TILE), :], local_sem.at[1 + j]
        )
        copy.start()
        rot.append(copy)
    own_r = pltpu.make_async_copy(
        right_roots.at[0, :, pl.ds(pl.multiple_of(g_of[0] * TILE, TILE), TILE), :],
        a_r.at[pl.ds(g_of[0] * NS, NS)],
        local_sem.at[6],
    )
    own_r.start()
    own_sec = pltpu.make_async_copy(second.at[0], sec, local_sem.at[7])
    own_sec.start()

    barrier = pltpu.get_barrier_semaphore()
    partners = [(d, (z + k) % NZ) for k in range(1, NZ)]
    partners += [(group(0, k)[1], z) for k in range(1, NG)]
    for k in range(1, NT):
        for cc in range(2):
            partners.append((((y + k) % 4) * 8 + x * 2 + cc, z))
    for p in partners:
        pl.semaphore_signal(barrier, inc=1, device_id=p, device_id_type=MESH)
    pl.semaphore_wait(barrier, len(partners))

    right, left = (z + 1) % NZ, (z + NZ - 1) % NZ

    def ring(buf, rows, ss, rs, first):
        part = rows // CH

        def copy(direction, s, c):
            slot = (z + NZ - s) % NZ if direction == 0 else (z + s) % NZ
            i = (direction * 4 + s) * CH + c
            span = pl.ds(c * part, part)
            src = first(span) if s == 0 else buf.at[slot, span, :]
            to = right if direction == 0 else left
            return remote(src, buf.at[slot, span, :], ss.at[i], rs.at[i], d, to)

        def last_dir(c):
            return 0 if c < CH // 2 else 1

        def begin():
            for c in range(CH):
                start(copy(0, 0, c))
                start(copy(1, 0, c))

        def relay(s):
            for c in range(CH):
                for direction in range(2):
                    copy(direction, s - 1, c).wait_recv()
                    if s < 3 or last_dir(c) == direction:
                        start(copy(direction, s, c))

        def finish():
            for c in range(CH):
                copy(last_dir(c), 3, c).wait_recv()

        return begin, relay, finish

    zg_begin, zg_relay, zg_finish = ring(gbuf, BS, zg_s, zg_r, lambda span: grads.at[0, span, :])
    zg_begin()

    for copy in rot:
        copy.wait()
    own_l = pltpu.make_async_copy(
        l_rot.at[:, pl.ds(pl.multiple_of(g_of[1] * PIECE, 16), PIECE), :],
        a_l.at[pl.ds(g_of[1] * NS, NS)],
        local_sem.at[8],
    )
    own_l.start()

    def s1(mode, k):
        g, to = group(mode, k)
        i = mode * NG + k
        if mode == 0:
            src = right_roots.at[0, :, pl.ds(pl.multiple_of(g * TILE, TILE), TILE), :]
        else:
            src = l_rot.at[:, pl.ds(pl.multiple_of(g * PIECE, 16), PIECE), :]
        dst = (a_r, a_l)[mode].at[pl.ds(g_of[mode] * NS, NS)]
        return remote(src, dst, s1_s.at[i], s1_r.at[i], to, z)

    for k in range(1, NG):
        start(s1(1, k))
        start(s1(0, k))

    own_g.wait()
    own_sec.wait()

    def adam_rows(i, total):
        rows = pl.ds(pl.multiple_of(i * TILE, TILE), TILE)
        g = gbuf[z, rows, :].astype(F32)
        new = beta_adam * sec[rows, :] + (1.0 - beta_adam) * g * g
        direction = g / (jnp.sqrt(new) + adam_eps)
        return total + jnp.sum((direction * direction).reshape(TILE // 8, 8, TILE), axis=0)

    adam_part = lax.fori_loop(0, BS // TILE, adam_rows, jnp.zeros((8, TILE), F32))

    def share(which, part):
        ps[which, z] = part
        copies = []
        for k in range(1, NZ):
            i = which * NZ + k
            copies.append(start(remote(ps.at[which, z], ps.at[which, z], ps_s.at[i], ps_r.at[i], d, (z + k) % NZ)))
        return copies

    adam_copies = share(0, adam_part)
    gt[...] = gbuf[z].T

    zg_relay(1)

    def s2(mode, k):
        t, to = other(mode, k)
        i = mode * NT + k
        dst = (b_r, b_l)[mode].at[pl.ds(t_of[mode] * NG, NG)]
        return remote((t_r, t_l)[mode].at[pl.ds((k - 1) * NG, NG)], dst, s2_s.at[i], s2_r.at[i], to, z)

    def s1_to_s2(mode):
        (own_r, own_l)[mode].wait()
        for k in range(1, NG):
            s1(mode, k).wait_recv()
        a, t_buf, b = ((a_r, t_r, b_r), (a_l, t_l, b_l))[mode]
        for k in (1, 3, 2, 0):
            t, _ = other(mode, k)

            def choose(g, _):
                index = tbl[mode, 0, dev(mode, g, t)]
                if k == 0:
                    b[t * NG + g] = a[index]
                else:
                    t_buf[(k - 1) * NG + g] = a[index]
                return 0

            lax.fori_loop(0, NG, choose, 0)
            if k:
                start(s2(mode, k))

    s1_to_s2(1)
    s1_to_s2(0)
    zg_relay(2)
    zg_relay(3)

    def s3(mode, k):
        g, to = group(mode, k)
        i = mode * NG + k
        dst = (d_r.at[g_of[mode]], d_l.at[pl.ds(pl.multiple_of(g_of[mode] * PIECE, 16), PIECE), :])[mode]
        return remote((c_r, c_l)[mode].at[k], dst, s3_s.at[i], s3_r.at[i], to, z)

    def s2_to_s3(mode):
        for k in range(1, NT):
            s2(mode, k).wait_recv()
        b, c_buf = ((b_r, c_r), (b_l, c_l))[mode]
        for k in range(NG):
            g, to = group(mode, k)
            value = b[tbl[mode, 1, to] * NG + g]
            if k:
                c_buf[k] = value
                start(s3(mode, k))
            elif mode == 0:
                d_r[g] = value
            else:
                d_l[pl.ds(pl.multiple_of(g * PIECE, 16), PIECE), :] = value

    def s3_done(mode):
        for k in range(1, NG):
            s3(mode, k).wait_recv()

    s2_to_s3(1)
    s2_to_s3(0)
    zg_finish()

    def g1(mode, k):
        g, to = group(mode, k)
        i = mode * NG + k
        dst = (f_r, f_l)[mode].at[t_of[mode] * NG + g_of[mode]]
        return remote((rg, lg)[mode].at[g], dst, g1_s.at[i], g1_r.at[i], to, z)

    def left_tile(i, _):
        total = jnp.zeros((TILE, TILE), F32)
        for c in range(NZ):
            own_rows = gbuf[c, pl.ds(pl.multiple_of(z * TILE, TILE), TILE), :]
            rows = gbuf[c, pl.ds(pl.multiple_of(i * TILE, TILE), TILE), :]
            total = total + dot(own_rows, rows, 1, 1)
        lg[i] = total.astype(BF16)
        return 0

    def right_tile(i, _):
        rg[i] = dot(gt[...], gbuf[i]).astype(BF16)
        return 0

    lax.fori_loop(0, NG, left_tile, 0)
    for k in range(1, NG):
        start(g1(1, k))
    f_l[t_of[1] * NG + g_of[1]] = lg[g_of[1]]
    lax.fori_loop(0, NG, right_tile, 0)
    for k in range(1, NG):
        start(g1(0, k))
    f_r[t_of[0] * NG + g_of[0]] = rg[g_of[0]]

    s3_done(1)
    zl_begin, zl_relay, zl_finish = ring(l_all, HALF, zl_s, zl_r, lambda span: d_l.at[span, :])
    zl_begin()

    s3_done(0)
    acc[...] = dot(gbuf[0], d_r[0])

    def mix(c, _):
        acc[...] += dot(gbuf[c], d_r[c])
        return 0

    lax.fori_loop(1, NZ, mix, 0)
    for j in range(11):
        mext[j] = acc[(j % NZ) * TILE:(j % NZ + 1) * TILE, :].astype(BF16)

    def g2(mode, k):
        t, to = other(mode, k)
        i = mode * NT + k
        mine = (f_r, f_l)[mode].at[pl.ds(t_of[mode] * NG, NG)]
        return remote(mine, mine, g2_s.at[i], g2_r.at[i], to, z)

    def g1_to_g2(mode):
        for k in range(1, NG):
            g1(mode, k).wait_recv()
        for k in (1, 3, 2):
            start(g2(mode, k))

    g1_to_g2(1)
    g1_to_g2(0)

    pre[...] = jnp.zeros((NZ, TILE, TILE), F32)

    def add_shard(shard, s):
        direct = dot(shard, mext[s])
        for j in range(5):
            row = (s + j) % NZ
            pre[row] += direct[j * TILE:(j + 1) * TILE, :]
        three = mext[pl.ds(s + 1, 3)].reshape(3 * TILE, TILE)
        pre[s] += dot(shard[TILE:4 * TILE, :], three, 0, 0)

    add_shard(d_l[...], z)
    zl_relay(1)
    add_shard(l_all[left], left)
    add_shard(l_all[right], right)
    zl_relay(2)

    def g3(mode, k):
        g, to = group(mode, k)
        i = mode * NG + k
        dst = (gram_r, gram_l)[mode].at[g_of[mode]]
        return remote((h_r, h_l)[mode].at[k], dst, g3_s.at[i], g3_r.at[i], to, z)

    def g2_to_g3(mode):
        for k in range(1, NT):
            g2(mode, k).wait_recv()
        f, h, out = ((f_r, h_r, gram_r), (f_l, h_l, gram_l))[mode]
        for k in range(NG):
            g, to = group(mode, k)
            for q in range(NS):
                value = f[tbl[mode, 2 + q, to]]
                if k:
                    h[k, q] = value
                else:
                    out[g, q] = value
            if k:
                start(g3(mode, k))

    add_shard(l_all[(z + 6) % NZ], (z + 6) % NZ)
    add_shard(l_all[(z + 2) % NZ], (z + 2) % NZ)
    zl_relay(3)
    g2_to_g3(1)
    g2_to_g3(0)
    add_shard(l_all[(z + 5) % NZ], (z + 5) % NZ)
    add_shard(l_all[(z + 3) % NZ], (z + 3) % NZ)
    zl_finish()
    add_shard(l_all[(z + 4) % NZ], (z + 4) % NZ)

    squares = jnp.zeros((8, TILE), F32)
    for a in range(NZ):
        rows = pre[a]
        squares = squares + jnp.sum((rows * rows).reshape(TILE // 8, 8, TILE), axis=0)
    norm_copies = share(1, squares)
    for copy in adam_copies + norm_copies:
        copy.wait_recv()

    def total(which):
        rows = jnp.sum(ps[which], axis=0)
        return jnp.sum(jnp.sum(rows, axis=0, keepdims=True), axis=1, keepdims=True)

    adam_sq = total(0).astype(BF16).astype(F32)
    scale = jnp.sqrt(adam_sq / (total(1) + norm_eps))
    for a in range(NZ):
        graft[a * TILE:(a + 1) * TILE, :] = (pre[a] * scale).astype(BF16)

    for mode in (1, 0):
        for k in range(1, NG):
            g3(mode, k).wait_recv()
    for copy in sent:
        copy.wait_send()


def update(filled, graft, momentum, gram_l, gram_r, left_stats, right_stats, step, momentum_out, left_out, right_out):
    new = beta_one * momentum[0] + (1.0 - beta_one) * graft[...].astype(F32)
    momentum_out[0] = new
    step[0] = (-step_rate * new).astype(BF16)
    for q in range(NS):
        on = filled[q] > 0
        for stats, gram, out in ((left_stats, gram_l, left_out), (right_stats, gram_r, right_out)):
            for c in range(NG):
                cols = slice(c * TILE, (c + 1) * TILE)
                term = jnp.where(on, gram[c, q].astype(F32), 0.0)
                out[0, q, :, cols] = beta_stat * stats[0, q, :, cols] + (1.0 - beta_stat) * term


def routes(owners):
    ids = jnp.arange(owners.shape[0], dtype=jnp.int32)
    same = owners[:, None] == owners[None, :]
    slot = jnp.sum((same & (ids[None, :] < ids[:, None])).astype(jnp.int32), axis=1)
    slots = jnp.arange(NS, dtype=jnp.int32)
    hit = (owners[None, None, :] == ids[None, :, None]) & (slot[None, None, :] == slots[:, None, None])
    block = jnp.sum(jnp.where(hit, ids[None, None, :], 0), axis=2)
    filled = jnp.any(hit, axis=2).astype(jnp.int32)

    def place(mode, i):
        if mode == 0:
            return i % 8, i // 8
        return (i // 8) * 2 + i % 2, (i // 2) % 4

    rows = []
    for mode in range(2):
        g, t = place(mode, owners)
        bg, bt = place(mode, block)
        rows.append(jnp.concatenate([(g * NS + slot)[None], t[None], bt * NG + bg], axis=0))
    return jnp.stack(rows), filled


def body(grads, momentum, second_moment, owners, left_stats, right_stats, left_roots, right_roots):
    tbl, filled = routes(owners)
    own = lax.dynamic_index_in_dim(filled, lax.axis_index("dp"), 1, keepdims=False)
    vmem = lambda shape, dtype=BF16: pltpu.VMEM(shape, dtype)
    dma = lambda n: pltpu.SemaphoreType.DMA((n,))
    any_spec = pl.BlockSpec(memory_space=pl.ANY)
    tile = (TILE, TILE)
    graft, gram_l, gram_r = pl.pallas_call(
        kernel,
        name="shampoo",
        out_shape=(
            jax.ShapeDtypeStruct((BS, TILE), BF16),
            jax.ShapeDtypeStruct((NG, NS) + tile, BF16),
            jax.ShapeDtypeStruct((NG, NS) + tile, BF16),
        ),
        in_specs=[pl.BlockSpec(memory_space=pltpu.SMEM)] + [any_spec] * 4,
        out_specs=[pl.BlockSpec(memory_space=pltpu.VMEM)] * 3,
        scratch_shapes=[
            vmem((NZ, BS, TILE)), vmem((BS, TILE), F32), vmem((NS, HALF, TILE)),
            vmem((NG * NS,) + tile), vmem((NG * NS, PIECE, TILE)),
            vmem((3 * NG,) + tile), vmem((3 * NG, PIECE, TILE)),
            vmem((NT * NG,) + tile), vmem((NT * NG, PIECE, TILE)),
            vmem((NG,) + tile), vmem((NG, PIECE, TILE)),
            vmem((NG,) + tile), vmem((HALF, TILE)),
            vmem((NZ, HALF, TILE)), vmem((NG,) + tile), vmem((NG,) + tile),
            vmem((NT * NG,) + tile), vmem((NT * NG,) + tile),
            vmem((NG, NS) + tile), vmem((NG, NS) + tile),
            vmem((BS, TILE), F32), vmem((11,) + tile), vmem((TILE, BS)), vmem((NZ,) + tile, F32), vmem((2, NZ, 8, TILE), F32),
            dma(9), dma(8 * CH), dma(8 * CH), dma(8 * CH), dma(8 * CH), dma(2 * NZ), dma(2 * NZ),
            dma(2 * NG), dma(2 * NG), dma(2 * NT), dma(2 * NT), dma(2 * NG), dma(2 * NG),
            dma(2 * NG), dma(2 * NG), dma(2 * NT), dma(2 * NT), dma(2 * NG), dma(2 * NG),
        ],
        compiler_params=pltpu.CompilerParams(collective_id=0, has_side_effects=True, vmem_limit_bytes=40 * 2**20),
    )(tbl, grads, second_moment, left_roots, right_roots)

    steps = 4
    rows, wide = TILE // steps, BS // steps
    slab = pl.BlockSpec((1, wide, TILE), lambda i: (0, i, 0))
    stats = pl.BlockSpec((1, NS, rows, BS), lambda i: (0, 0, i, 0))
    gram = pl.BlockSpec((NG, NS, rows, TILE), lambda i: (0, 0, i, 0))
    return pl.pallas_call(
        update,
        name="update",
        grid=(steps,),
        out_shape=(
            jax.ShapeDtypeStruct((1, BS, TILE), BF16),
            jax.ShapeDtypeStruct((1, BS, TILE), F32),
            jax.ShapeDtypeStruct((1, NS, TILE, BS), F32),
            jax.ShapeDtypeStruct((1, NS, TILE, BS), F32),
        ),
        in_specs=[
            pl.BlockSpec(memory_space=pltpu.SMEM),
            pl.BlockSpec((wide, TILE), lambda i: (i, 0)),
            slab, gram, gram, stats, stats,
        ],
        out_specs=(slab, slab, stats, stats),
        compiler_params=pltpu.CompilerParams(vmem_limit_bytes=40 * 2**20),
    )(own, graft, momentum, gram_l, gram_r, left_stats, right_stats)


def solution(mesh):
    return jax.shard_map(
        body,
        mesh=mesh,
        in_specs=(
            P("dp", None, "mp"),
            P("dp", None, "mp"),
            P("dp", None, "mp"),
            P(),
            P("dp", None, "mp", None),
            P("dp", None, "mp", None),
            P("dp", None, None, "mp"),
            P("dp", None, None, "mp"),
        ),
        out_specs=(
            P("dp", None, "mp"),
            P("dp", None, "mp"),
            P("dp", None, "mp", None),
            P("dp", None, "mp", None),
        ),
        check_vma=False,
    )
```

```python
import jax
import jax.numpy as jnp
from jax import lax
from jax.experimental import pallas as pl
from jax.experimental.pallas import tpu as pltpu
from jax.sharding import PartitionSpec as P

beta_one = 0.9
beta_adam = 0.99
beta_stat = 0.95
adam_eps = 1e-08
norm_eps = 1e-06
step_rate = 0.5

MESH = pl.DeviceIdType.MESH
NZ = 8
NG = 8
NT = 4
NBLK = 32
NS = 3
TILE = 128
BS = 1024
HALF = 5 * TILE
PIECE = HALF // NG
CH = 2
F32 = jnp.float32
BF16 = jnp.bfloat16


def dot(a, b, ca=1, cb=0):
    return lax.dot_general(a, b, (((ca,), (cb,)), ((), ())), preferred_element_type=F32)


def place(mode, i):
    if mode == 0:
        return i & 7, i >> 3
    return (i >> 3) * 2 + (i & 1), (i >> 1) & 3


def kernel(
    owners, grads, second, left_roots, right_roots,
    graft, gram_l, gram_r,
    gbuf, sec, rot, a_r, a_l, t_buf, b_r, b_l, c_buf, strip, cross,
    l_all, gram, f_r, f_l, h, lacc, acc, mext, gt, pre, ps,
    slot_of, source, local_sem, xr_s, xr_r, zg_s, zg_r, zl_s, zl_r, ps_s, ps_r, s1_s, s1_r, s2_s, s2_r, s3_s, s3_r, g1_s, g1_r, g2_s, g2_r, g3_s, g3_r,
):
    a, b, f = (a_r, a_l), (b_r, b_l), (f_r, f_l)
    d = lax.axis_index("dp")
    z = lax.axis_index("mp")
    core = d % 2
    x = (d // 2) % 4
    y = d // 8

    g_of = (x * 2 + core, y * 2 + core)
    t_of = (y, x)

    def dev(mode, g, t):
        if mode == 0:
            return t * 8 + g
        return (g // 2) * 8 + t * 2 + g % 2

    def group(mode, k):
        g = (g_of[mode] + k) % NG
        return g, dev(mode, g, t_of[mode])

    def other(mode, k):
        t = (t_of[mode] + k) % NT
        return t, dev(mode, g_of[mode], t)

    def remote(src, dst, ss, rs, i, to, zto):
        return pltpu.make_async_remote_copy(
            src_ref=src, dst_ref=dst, send_sem=ss.at[i], recv_sem=rs.at[i], device_id=(to, zto), device_id_type=MESH
        )

    sent = []

    def start(copy):
        copy.start()
        sent.append(copy)
        return copy

    barrier = pltpu.get_barrier_semaphore()
    partners = [(d, (z + k) % NZ) for k in range(1, NZ)]
    partners += [(group(0, k)[1], z) for k in range(1, NG)]
    for k in range(1, NT):
        for cc in range(2):
            partners.append((((y + k) % 4) * 8 + x * 2 + cc, z))
    for p in partners:
        pl.semaphore_signal(barrier, inc=1, device_id=p, device_id_type=MESH)
    own_g = pltpu.make_async_copy(grads.at[0], gbuf.at[z], local_sem.at[0])
    own_g.start()
    strips = []
    for mode in (1, 0):
        for j in range(5):
            row = pl.multiple_of(((z + j) % NZ) * TILE, TILE)
            copy = pltpu.make_async_copy(
                (right_roots, left_roots)[mode].at[0, :, pl.ds(row, TILE), :],
                rot.at[mode, :, pl.ds(j * TILE, TILE), :],
                local_sem.at[4 + 5 * mode + j],
            )
            copy.start()
            strips.append(copy)
    own_sec = pltpu.make_async_copy(second.at[0], sec, local_sem.at[1])
    own_sec.start()

    pl.semaphore_wait(barrier, len(partners))

    right, left = (z + 1) % NZ, (z + NZ - 1) % NZ

    def ring(buf, rows, ss, rs, first):
        part = rows // CH

        def copy(direction, s, c):
            slot = (z + NZ - s) % NZ if direction == 0 else (z + s) % NZ
            i = (direction * 4 + s) * CH + c
            span = pl.ds(c * part, part)
            src = first(span) if s == 0 else buf.at[slot, span, :]
            to = right if direction == 0 else left
            return remote(src, buf.at[slot, span, :], ss, rs, i, d, to)

        def last_dir(c):
            return 0 if c < CH // 2 else 1

        def begin():
            for c in range(CH):
                start(copy(0, 0, c))
                start(copy(1, 0, c))

        def relay(s):
            for c in range(CH):
                for direction in range(2):
                    copy(direction, s - 1, c).wait_recv()
                    if s < 3 or last_dir(c) == direction:
                        start(copy(direction, s, c))

        def finish():
            for c in range(CH):
                copy(last_dir(c), 3, c).wait_recv()

        return begin, relay, finish

    zg_begin, zg_relay, zg_finish = ring(gbuf, BS, zg_s, zg_r, lambda span: grads.at[0, span, :])
    zg_begin()

    def find_slot(b, _):
        count = jnp.int32(0)
        for c in range(NBLK):
            count += jnp.where((owners[c] == owners[b]) & (c < b), 1, 0)
        slot_of[b] = jnp.minimum(count, NS - 1)
        return 0

    def find_blocks(i, _):
        for mode in range(2):
            o = dev(mode, i, t_of[mode])
            found = [jnp.int32(0)] * NS
            for b in range(NBLK):
                g, t = place(mode, b)
                mine = owners[b] == o
                for q in range(NS):
                    found[q] = jnp.where(mine & (slot_of[b] == q), t * NG + g, found[q])
            for q in range(NS):
                source[mode, i * NS + q] = found[q]
        return 0

    def piece(g):
        return pl.ds(pl.multiple_of(g * PIECE, 16), PIECE)

    def s1(mode, k):
        g, to = group(mode, k)
        dst = a[mode].at[pl.ds(g_of[mode] * NS, NS)]
        return remote(rot.at[mode, :, piece(g), :], dst, s1_s, s1_r, mode * NG + k, to, z)

    for copy in strips:
        copy.wait()
    own_pieces = []
    for mode in range(2):
        own_pieces.append(
            pltpu.make_async_copy(
                rot.at[mode, :, piece(g_of[mode]), :], a[mode].at[pl.ds(g_of[mode] * NS, NS)], local_sem.at[2 + mode]
            )
        )
        own_pieces[mode].start()
    for k in range(1, NG):
        start(s1(1, k))
        start(s1(0, k))

    own_g.wait()
    own_sec.wait()

    def adam_rows(i, total):
        rows = pl.ds(pl.multiple_of(i * TILE, TILE), TILE)
        g = gbuf[z, rows, :].astype(F32)
        new = beta_adam * sec[rows, :] + (1.0 - beta_adam) * g * g
        direction = g / (jnp.sqrt(new) + adam_eps)
        return total + jnp.sum((direction * direction).reshape(TILE // 8, 8, TILE), axis=0)

    adam_part = lax.fori_loop(0, BS // TILE, adam_rows, jnp.zeros((8, TILE), F32))

    def share(which, part):
        ps[which, z] = part
        copies = []
        for k in range(1, NZ):
            i = which * NZ + k
            copies.append(start(remote(ps.at[which, z], ps.at[which, z], ps_s, ps_r, i, d, (z + k) % NZ)))
        return copies

    adam_copies = share(0, adam_part)
    lax.fori_loop(0, NBLK, find_slot, 0)
    gt[...] = gbuf[z].T
    own_rows = pl.ds(pl.multiple_of(z * TILE, TILE), TILE)

    def add_gram(shard, first=False):
        gram[0, shard] = dot(gt[...], gbuf[shard]).astype(BF16)
        term = dot(gbuf[shard, own_rows, :], gbuf[shard], 1, 1)
        lacc[...] = term if first else lacc[...] + term

    add_gram(z, True)
    zg_relay(1)

    def s2(mode, k):
        t, to = other(mode, k)
        dst = b[mode].at[pl.ds(t_of[mode] * NG, NG)]
        return remote(t_buf.at[mode, pl.ds((k - 1) * NG, NG)], dst, s2_s, s2_r, mode * NT + k, to, z)

    def s1_to_s2(mode):
        own_pieces[mode].wait()
        for k in range(1, NG):
            s1(mode, k).wait_recv()
        for k in (1, 3, 2, 0):
            t, _ = other(mode, k)

            def choose(g, _):
                b_id = dev(mode, g, t)
                value = a[mode][place(mode, owners[b_id])[0] * NS + slot_of[b_id]]
                if k == 0:
                    b[mode][t * NG + g] = value
                else:
                    t_buf[mode, (k - 1) * NG + g] = value
                return 0

            lax.fori_loop(0, NG, choose, 0)
            if k:
                start(s2(mode, k))

    s1_to_s2(1)
    s1_to_s2(0)
    lax.fori_loop(0, NG, find_blocks, 0)
    add_gram(left)
    add_gram(right)
    zg_relay(2)
    add_gram((z + 6) % NZ)
    add_gram((z + 2) % NZ)
    zg_relay(3)
    add_gram((z + 5) % NZ)
    add_gram((z + 3) % NZ)

    def s3(mode, k):
        g, to = group(mode, k)
        return remote(
            c_buf.at[mode, k], strip.at[mode, piece(g_of[mode]), :], s3_s, s3_r, mode * NG + k, to, z
        )

    def s2_to_s3(mode):
        for k in range(1, NT):
            s2(mode, k).wait_recv()
        for k in range(NG):
            g, to = group(mode, k)
            value = b[mode][place(mode, owners[to])[1] * NG + g]
            if k:
                c_buf[mode, k] = value
                start(s3(mode, k))
            else:
                strip[mode, piece(g), :] = value

    def s3_done(mode):
        for k in range(1, NG):
            s3(mode, k).wait_recv()

    s2_to_s3(1)
    s2_to_s3(0)
    zg_finish()
    add_gram((z + 4) % NZ)

    def g1(mode, k):
        g, to = group(mode, k)
        dst = f[mode].at[t_of[mode] * NG + g_of[mode]]
        return remote(gram.at[mode, g], dst, g1_s, g1_r, mode * NG + k, to, z)

    for g in range(NG):
        gram[1, g] = lacc[:, g * TILE:(g + 1) * TILE].astype(BF16)
    for k in range(NG):
        for mode in range(2):
            g, _ = group(mode, k)
            if k:
                start(g1(mode, k))
            else:
                f[mode][t_of[mode] * NG + g] = gram[mode, g]

    def xr(j):
        return remote(strip.at[0, pl.ds(j * TILE, TILE), :], cross.at[j - 1], xr_s, xr_r, j, d, (z + j) % NZ)

    s3_done(0)
    for j in (1, 2, 3):
        start(xr(j))

    s3_done(1)
    zl_begin, zl_relay, zl_finish = ring(l_all, HALF, zl_s, zl_r, lambda span: strip.at[1, span, :])
    zl_begin()

    def g2(mode, direction, kind):
        k = 1 - 2 * direction
        _, to = other(mode, k + NT)
        half = direction if kind != 1 else 1 - direction
        t = t_of[mode] if kind < 2 else (t_of[mode] + NT - k) % NT
        span = f[mode].at[pl.ds(t * NG + half * (NG // 2), NG // 2)]
        return remote(span, span, g2_s, g2_r, (mode * 2 + direction) * 3 + kind, to, z)

    def g2_begin(mode):
        for k in range(1, NG):
            g1(mode, k).wait_recv()
        for kind in range(2):
            for direction in range(2):
                start(g2(mode, direction, kind))

    def g2_relay(mode):
        for direction in range(2):
            g2(mode, direction, 0).wait_recv()
            start(g2(mode, direction, 2))

    def g2_finish(mode):
        for direction in range(2):
            for kind in (1, 2):
                g2(mode, direction, kind).wait_recv()

    g2_begin(1)
    g2_begin(0)

    acc[...] = dot(gbuf[z], strip[0, 0:TILE, :])
    for j in range(1, 5):
        acc[...] += dot(gbuf[(z + j) % NZ], strip[0, j * TILE:(j + 1) * TILE, :])
    for j in (1, 2, 3):
        xr(j).wait_recv()
        acc[...] += dot(gbuf[(z + NZ - j) % NZ], cross[j - 1], 1, 1)
    for j in range(11):
        mext[j] = acc[(j % NZ) * TILE:(j % NZ + 1) * TILE, :].astype(BF16)

    pre[...] = jnp.zeros((NZ, TILE, TILE), F32)

    def add_shard(shard, s):
        direct = dot(shard, mext[s])
        for j in range(5):
            row = (s + j) % NZ
            pre[row] += direct[j * TILE:(j + 1) * TILE, :]
        three = mext[pl.ds(s + 1, 3)].reshape(3 * TILE, TILE)
        pre[s] += dot(shard[TILE:4 * TILE, :], three, 0, 0)

    zl_relay(1)
    g2_relay(1)
    g2_relay(0)
    add_shard(strip[1], z)
    zl_relay(2)
    add_shard(l_all[left], left)
    add_shard(l_all[right], right)

    def g3(mode, k):
        g, to = group(mode, k)
        dst = (gram_r, gram_l)[mode].at[g_of[mode]]
        return remote(h.at[mode, k], dst, g3_s, g3_r, mode * NG + k, to, z)

    def g2_to_g3(mode):
        g2_finish(mode)
        out = (gram_r, gram_l)[mode]
        for k in range(NG):
            g, to = group(mode, k)
            for q in range(NS):
                value = f[mode][source[mode, g * NS + q]]
                if k:
                    h[mode, k, q] = value
                else:
                    out[g, q] = value
            if k:
                start(g3(mode, k))

    zl_relay(3)
    g2_to_g3(1)
    g2_to_g3(0)
    add_shard(l_all[(z + 6) % NZ], (z + 6) % NZ)
    add_shard(l_all[(z + 2) % NZ], (z + 2) % NZ)
    add_shard(l_all[(z + 5) % NZ], (z + 5) % NZ)
    add_shard(l_all[(z + 3) % NZ], (z + 3) % NZ)
    zl_finish()
    add_shard(l_all[(z + 4) % NZ], (z + 4) % NZ)

    squares = jnp.zeros((8, TILE), F32)
    for a in range(NZ):
        rows = pre[a]
        squares = squares + jnp.sum((rows * rows).reshape(TILE // 8, 8, TILE), axis=0)
    norm_copies = share(1, squares)
    for copy in adam_copies + norm_copies:
        copy.wait_recv()

    def total(which):
        rows = jnp.sum(ps[which], axis=0)
        return jnp.sum(jnp.sum(rows, axis=0, keepdims=True), axis=1, keepdims=True)

    adam_sq = total(0).astype(BF16).astype(F32)
    scale = jnp.sqrt(adam_sq / (total(1) + norm_eps))
    for a in range(NZ):
        graft[a * TILE:(a + 1) * TILE, :] = (pre[a] * scale).astype(BF16)

    for mode in (1, 0):
        for k in range(1, NG):
            g3(mode, k).wait_recv()
    for copy in sent:
        copy.wait_send()


def update(owners, graft, momentum, gram_l, gram_r, left_stats, right_stats, step, momentum_out, left_out, right_out):
    new = beta_one * momentum[0] + (1.0 - beta_one) * graft[...].astype(F32)
    momentum_out[0] = new
    step[0] = (-step_rate * new).astype(BF16)
    own = lax.axis_index("dp")
    count = jnp.int32(0)
    for b in range(NBLK):
        count += jnp.where(owners[b] == own, 1, 0)
    for q in range(NS):
        on = count > q
        for stats, gram, out in ((left_stats, gram_l, left_out), (right_stats, gram_r, right_out)):
            for c in range(NG):
                cols = slice(c * TILE, (c + 1) * TILE)
                term = jnp.where(on, gram[c, q].astype(F32), 0.0)
                out[0, q, :, cols] = beta_stat * stats[0, q, :, cols] + (1.0 - beta_stat) * term


def body(grads, momentum, second_moment, owners, left_stats, right_stats, left_roots, right_roots):
    vmem = lambda shape, dtype=BF16: pltpu.VMEM(shape, dtype)
    dma = lambda n: pltpu.SemaphoreType.DMA((n,))
    hbm = pl.BlockSpec(memory_space=pltpu.MemorySpace.HBM)
    tile = (TILE, TILE)
    graft, gram_l, gram_r = pl.pallas_call(
        kernel,
        name="shampoo",
        out_shape=(
            jax.ShapeDtypeStruct((BS, TILE), BF16),
            jax.ShapeDtypeStruct((NG, NS) + tile, BF16),
            jax.ShapeDtypeStruct((NG, NS) + tile, BF16),
        ),
        in_specs=[pl.BlockSpec(memory_space=pltpu.SMEM)] + [hbm] * 4,
        out_specs=[pl.BlockSpec(memory_space=pltpu.VMEM)] * 3,
        scratch_shapes=[
            vmem((NZ, BS, TILE)), vmem((BS, TILE), F32), vmem((2, NS, HALF, TILE)),
            vmem((NG * NS, PIECE, TILE)), vmem((NG * NS, PIECE, TILE)), vmem((2, 3 * NG, PIECE, TILE)),
            vmem((NT * NG, PIECE, TILE)), vmem((NT * NG, PIECE, TILE)),
            vmem((2, NG, PIECE, TILE)), vmem((2, HALF, TILE)), vmem((3,) + tile),
            vmem((NZ, HALF, TILE)), vmem((2, NG) + tile), vmem((NT * NG,) + tile), vmem((NT * NG,) + tile), vmem((2, NG, NS) + tile),
            vmem((TILE, BS), F32), vmem((BS, TILE), F32), vmem((11,) + tile), vmem((TILE, BS)),
            vmem((NZ,) + tile, F32), vmem((2, NZ, 8, TILE), F32),
            pltpu.SMEM((NBLK,), jnp.int32), pltpu.SMEM((2, NG * NS), jnp.int32),
            dma(14), dma(4), dma(4), dma(8 * CH), dma(8 * CH), dma(8 * CH), dma(8 * CH), dma(2 * NZ), dma(2 * NZ),
            dma(2 * NG), dma(2 * NG), dma(2 * NT), dma(2 * NT), dma(2 * NG), dma(2 * NG),
            dma(2 * NG), dma(2 * NG), dma(12), dma(12), dma(2 * NG), dma(2 * NG),
        ],
        compiler_params=pltpu.CompilerParams(collective_id=0, has_side_effects=True, vmem_limit_bytes=60 * 2**20),
    )(owners, grads, second_moment, left_roots, right_roots)

    steps = 2
    rows, wide = TILE // steps, BS // steps
    slab = pl.BlockSpec((1, wide, TILE), lambda i: (0, i, 0))
    stats = pl.BlockSpec((1, NS, rows, BS), lambda i: (0, 0, i, 0))
    gram = pl.BlockSpec((NG, NS, rows, TILE), lambda i: (0, 0, i, 0))
    return pl.pallas_call(
        update,
        name="update",
        grid=(steps,),
        out_shape=(
            jax.ShapeDtypeStruct((1, BS, TILE), BF16),
            jax.ShapeDtypeStruct((1, BS, TILE), F32),
            jax.ShapeDtypeStruct((1, NS, TILE, BS), F32),
            jax.ShapeDtypeStruct((1, NS, TILE, BS), F32),
        ),
        in_specs=[
            pl.BlockSpec(memory_space=pltpu.SMEM),
            pl.BlockSpec((wide, TILE), lambda i: (i, 0)),
            slab, gram, gram, stats, stats,
        ],
        out_specs=(slab, slab, stats, stats),
        compiler_params=pltpu.CompilerParams(vmem_limit_bytes=60 * 2**20),
    )(owners, graft, momentum, gram_l, gram_r, left_stats, right_stats)


def solution(mesh):
    return jax.shard_map(
        body,
        mesh=mesh,
        in_specs=(
            P("dp", None, "mp"),
            P("dp", None, "mp"),
            P("dp", None, "mp"),
            P(),
            P("dp", None, "mp", None),
            P("dp", None, "mp", None),
            P("dp", None, None, "mp"),
            P("dp", None, None, "mp"),
        ),
        out_specs=(
            P("dp", None, "mp"),
            P("dp", None, "mp"),
            P("dp", None, "mp", None),
            P("dp", None, "mp", None),
        ),
        check_vma=False,
    )
```

```python
import jax
import jax.numpy as jnp
from jax import lax
from jax.experimental import pallas as pl
from jax.experimental.pallas import tpu as pltpu
from jax.sharding import PartitionSpec as P

beta_one = 0.9
beta_adam = 0.99
beta_stat = 0.95
adam_eps = 1e-08
norm_eps = 1e-06
step_rate = 0.5

MESH = pl.DeviceIdType.MESH
NZ = 8
NG = 8
NT = 4
NBLK = 32
NS = 3
TILE = 128
BS = 1024
HALF = 5 * TILE
PIECE = HALF // NG
CH = 2
F32 = jnp.float32
BF16 = jnp.bfloat16


def dot(a, b, ca=1, cb=0):
    return lax.dot_general(a, b, (((ca,), (cb,)), ((), ())), preferred_element_type=F32)


def place(mode, i):
    if mode == 0:
        return i & 7, i >> 3
    return (i >> 3) * 2 + (i & 1), (i >> 1) & 3


def kernel(
    owners, grads, second, left_roots, right_roots,
    graft, gram_l, gram_r,
    gbuf, sec, rot, a_r, a_l, t_buf, b_r, b_l, via, c_buf, strip, cross,
    l_all, gram, f_r, f_l, h, lacc, acc, mext, gt, pre, ps, grafted,
    slot_of, source, local_sem, xr_s, xr_r, zg_s, zg_r, zl_s, zl_r, ps_s, ps_r, s1_s, s1_r, s2_s, s2_r, s3_s, s3_r, g1_s, g1_r, g2_s, g2_r, g3_s, g3_r,
):
    a, b, f = (a_r, a_l), (b_r, b_l), (f_r, f_l)
    d = lax.axis_index("dp")
    z = lax.axis_index("mp")
    core = d % 2
    x = (d // 2) % 4
    y = d // 8

    g_of = (x * 2 + core, y * 2 + core)
    t_of = (y, x)

    def dev(mode, g, t):
        if mode == 0:
            return t * 8 + g
        return (g // 2) * 8 + t * 2 + g % 2

    def group(mode, k):
        g = (g_of[mode] + k) % NG
        return g, dev(mode, g, t_of[mode])

    def other(mode, k):
        t = (t_of[mode] + k) % NT
        return t, dev(mode, g_of[mode], t)

    def remote(src, dst, ss, rs, i, to, zto):
        return pltpu.make_async_remote_copy(
            src_ref=src, dst_ref=dst, send_sem=ss.at[i], recv_sem=rs.at[i], device_id=(to, zto), device_id_type=MESH
        )

    sent = []

    def start(copy):
        copy.start()
        sent.append(copy)
        return copy

    barrier = pltpu.get_barrier_semaphore()
    partners = [(d, (z + k) % NZ) for k in (1, 7)]
    partners += [(group(0, k)[1], z) for k in range(1, NG)]
    for k in range(1, NT):
        for cc in range(2):
            partners.append((((y + k) % 4) * 8 + x * 2 + cc, z))
    for p in partners:
        pl.semaphore_signal(barrier, inc=1, device_id=p, device_id_type=MESH)
    def flush():
        for copy in sent:
            copy.wait_send()
        sent.clear()

    strips = []
    for mode in (1, 0):
        for j in range(5):
            row = pl.multiple_of(((z + j) % NZ) * TILE, TILE)
            copy = pltpu.make_async_copy(
                (right_roots, left_roots)[mode].at[0, :, pl.ds(row, TILE), :],
                rot.at[mode, :, pl.ds(j * TILE, TILE), :],
                local_sem.at[4 + 5 * mode + j],
            )
            copy.start()
            strips.append(copy)
    own_g = pltpu.make_async_copy(grads.at[0], gbuf.at[z], local_sem.at[0])
    own_g.start()
    own_sec = pltpu.make_async_copy(second.at[0], sec, local_sem.at[1])
    own_sec.start()

    pl.semaphore_wait(barrier, len(partners))

    right, left = (z + 1) % NZ, (z + NZ - 1) % NZ

    def ring(buf, rows, ss, rs, first):
        part = rows // CH

        def copy(direction, s, c):
            slot = (z + NZ - s) % NZ if direction == 0 else (z + s) % NZ
            i = (direction * 4 + s) * CH + c
            span = pl.ds(c * part, part)
            src = first(span) if s == 0 else buf.at[slot, span, :]
            to = right if direction == 0 else left
            return remote(src, buf.at[slot, span, :], ss, rs, i, d, to)

        def last_dir(c):
            return 0 if c < CH // 2 else 1

        def begin():
            for c in range(CH):
                start(copy(0, 0, c))
                start(copy(1, 0, c))

        def relay(s):
            for c in range(CH):
                for direction in range(2):
                    copy(direction, s - 1, c).wait_recv()
                    if s < 3 or last_dir(c) == direction:
                        start(copy(direction, s, c))

        def finish():
            for c in range(CH):
                copy(last_dir(c), 3, c).wait_recv()

        return begin, relay, finish

    zg_begin, zg_relay, zg_finish = ring(gbuf, BS, zg_s, zg_r, lambda span: grads.at[0, span, :])
    zg_begin()

    def find_slot(b, _):
        count = jnp.int32(0)
        for c in range(NBLK):
            count += jnp.where((owners[c] == owners[b]) & (c < b), 1, 0)
        slot_of[b] = jnp.minimum(count, NS - 1)
        return 0

    def find_blocks(i, _):
        for mode in range(2):
            o = dev(mode, i, t_of[mode])
            found = [jnp.int32(0)] * NS
            for b in range(NBLK):
                g, t = place(mode, b)
                mine = owners[b] == o
                for q in range(NS):
                    found[q] = jnp.where(mine & (slot_of[b] == q), t * NG + g, found[q])
            for q in range(NS):
                source[mode, i * NS + q] = found[q]
        return 0

    def piece(g):
        return pl.ds(pl.multiple_of(g * PIECE, 16), PIECE)

    def s1(mode, k):
        g, to = group(mode, k)
        dst = a[mode].at[pl.ds(g_of[mode] * NS, NS)]
        return remote(rot.at[mode, :, piece(g), :], dst, s1_s, s1_r, mode * NG + k, to, z)

    for copy in strips:
        copy.wait()
    own_pieces = []
    for mode in range(2):
        own_pieces.append(
            pltpu.make_async_copy(
                rot.at[mode, :, piece(g_of[mode]), :], a[mode].at[pl.ds(g_of[mode] * NS, NS)], local_sem.at[2 + mode]
            )
        )
        own_pieces[mode].start()
    for k in range(1, NG):
        start(s1(1, k))
        start(s1(0, k))

    own_g.wait()
    own_sec.wait()

    def adam_rows(i, total):
        rows = pl.ds(pl.multiple_of(i * TILE, TILE), TILE)
        g = gbuf[z, rows, :].astype(F32)
        new = beta_adam * sec[rows, :] + (1.0 - beta_adam) * g * g
        direction = g / (jnp.sqrt(new) + adam_eps)
        return total + jnp.sum((direction * direction).reshape(TILE // 8, 8, TILE), axis=0)

    adam_part = lax.fori_loop(0, BS // TILE, adam_rows, jnp.zeros((8, TILE), F32))

    ps[z, 0] = adam_part
    lax.fori_loop(0, NBLK, find_slot, 0)
    gt[...] = gbuf[z].T
    own_rows = pl.ds(pl.multiple_of(z * TILE, TILE), TILE)

    def add_gram(shard, first=False):
        gram[0, shard] = dot(gt[...], gbuf[shard]).astype(BF16)
        term = dot(gbuf[shard, own_rows, :], gbuf[shard], 1, 1)
        lacc[...] = term if first else lacc[...] + term

    add_gram(z, True)
    zg_relay(1)

    def s2(mode, direction, kind):
        _, to = other(mode, 1 - 2 * direction + NT)
        half = (direction, 1 - direction, direction)[kind] * (NG // 2)
        src = (16, 8 * direction, 8 * direction)[kind] + half
        if kind == 0:
            dst = via.at[mode, direction]
        else:
            dst = b[mode].at[pl.ds(8 + 8 * direction + half, NG // 2)]
        i = (mode * 2 + direction) * 3 + kind
        return remote(t_buf.at[mode, pl.ds(src, NG // 2)], dst, s2_s, s2_r, i, to, z)

    def candidate(mode, g, t):
        b_id = dev(mode, g, t)
        g_owner, t_owner = place(mode, owners[b_id])
        return a[mode][g_owner * NS + slot_of[b_id]], t_owner

    def s1_to_s2(mode):
        own_pieces[mode].wait()
        for k in range(1, NG):
            s1(mode, k).wait_recv()
        opposite, _ = other(mode, 2)
        for direction in range(2):
            for g in range(4 * direction, 4 * direction + 4):
                t_buf[mode, 16 + g] = candidate(mode, g, opposite)[0]
            start(s2(mode, direction, 0))
        for direction in range(2):
            t, _ = other(mode, 1 - 2 * direction + NT)
            for g in range(4 - 4 * direction, 8 - 4 * direction):
                t_buf[mode, 8 * direction + g] = candidate(mode, g, t)[0]
            start(s2(mode, direction, 1))
        for g in range(NG):
            b[mode][g] = candidate(mode, g, t_of[mode])[0]

    def s2_merge(mode):
        for direction in range(2):
            s2(mode, direction, 0).wait_recv()
            k = 1 - 2 * direction
            t, _ = other(mode, k + NT)
            behind, _ = other(mode, NT - k)
            for i in range(4):
                g = 4 * direction + i
                value, t_owner = candidate(mode, g, t)
                t_buf[mode, 8 * direction + g] = jnp.where(t_owner == behind, via[mode, direction, i], value)
            start(s2(mode, direction, 2))

    s1_to_s2(1)
    s1_to_s2(0)
    lax.fori_loop(0, NG, find_blocks, 0)
    add_gram(left)
    add_gram(right)
    zg_relay(2)
    s2_merge(1)
    s2_merge(0)
    add_gram((z + 6) % NZ)
    add_gram((z + 2) % NZ)
    flush()
    zg_relay(3)
    add_gram((z + 5) % NZ)
    add_gram((z + 3) % NZ)

    def s3(mode, k):
        g, to = group(mode, k)
        return remote(
            c_buf.at[mode, k], strip.at[mode, piece(g_of[mode]), :], s3_s, s3_r, mode * NG + k, to, z
        )

    def s2_to_s3(mode):
        for direction in range(2):
            for kind in (1, 2):
                s2(mode, direction, kind).wait_recv()
        for k in range(NG):
            g, to = group(mode, k)
            steps = (place(mode, owners[to])[1] + NT - t_of[mode]) % NT
            side = jnp.where(steps == 3, 1, jnp.where(steps == 1, 2, jnp.where(g < 4, 1, 2)))
            value = b[mode][jnp.where(steps == 0, 0, side) * NG + g]
            if k:
                c_buf[mode, k] = value
                start(s3(mode, k))
            else:
                strip[mode, piece(g), :] = value

    def s3_done(mode):
        for k in range(1, NG):
            s3(mode, k).wait_recv()

    s2_to_s3(1)
    s2_to_s3(0)
    zg_finish()
    add_gram((z + 4) % NZ)

    def g1(mode, k):
        g, to = group(mode, k)
        dst = f[mode].at[t_of[mode] * NG + g_of[mode]]
        return remote(gram.at[mode, g], dst, g1_s, g1_r, mode * NG + k, to, z)

    for g in range(NG):
        gram[1, g] = lacc[:, g * TILE:(g + 1) * TILE].astype(BF16)
    for k in range(NG):
        for mode in range(2):
            g, _ = group(mode, k)
            if k:
                start(g1(mode, k))
            else:
                f[mode][t_of[mode] * NG + g] = gram[mode, g]

    def xr(j):
        return remote(strip.at[0, pl.ds(j * TILE, TILE), :], cross.at[j - 1], xr_s, xr_r, j, d, (z + j) % NZ)

    s3_done(0)
    for j in (1, 2, 3):
        start(xr(j))

    s3_done(1)
    zl_begin, zl_relay, zl_finish = ring(l_all, HALF, zl_s, zl_r, lambda span: strip.at[1, span, :])
    zl_begin()

    def g2(mode, direction, kind):
        k = 1 - 2 * direction
        _, to = other(mode, k + NT)
        half = direction if kind != 1 else 1 - direction
        t = t_of[mode] if kind < 2 else (t_of[mode] + NT - k) % NT
        span = f[mode].at[pl.ds(t * NG + half * (NG // 2), NG // 2)]
        return remote(span, span, g2_s, g2_r, (mode * 2 + direction) * 3 + kind, to, z)

    def g2_begin(mode):
        for k in range(1, NG):
            g1(mode, k).wait_recv()
        for kind in range(2):
            for direction in range(2):
                start(g2(mode, direction, kind))

    def g2_relay(mode):
        for direction in range(2):
            g2(mode, direction, 0).wait_recv()
            start(g2(mode, direction, 2))

    def g2_finish(mode):
        for direction in range(2):
            for kind in (1, 2):
                g2(mode, direction, kind).wait_recv()

    flush()
    g2_begin(1)
    g2_begin(0)

    acc[...] = dot(gbuf[z], strip[0, 0:TILE, :])
    for j in range(1, 5):
        acc[...] += dot(gbuf[(z + j) % NZ], strip[0, j * TILE:(j + 1) * TILE, :])
    for j in (1, 2, 3):
        xr(j).wait_recv()
        acc[...] += dot(gbuf[(z + NZ - j) % NZ], cross[j - 1], 1, 1)
    for j in range(11):
        mext[j] = acc[(j % NZ) * TILE:(j % NZ + 1) * TILE, :].astype(BF16)

    pre[...] = jnp.zeros((NZ, TILE, TILE), F32)

    def add_shard(shard, s):
        direct = dot(shard, mext[s])
        for j in range(5):
            row = (s + j) % NZ
            pre[row] += direct[j * TILE:(j + 1) * TILE, :]
        three = mext[pl.ds(s + 1, 3)].reshape(3 * TILE, TILE)
        pre[s] += dot(shard[TILE:4 * TILE, :], three, 0, 0)

    zl_relay(1)
    g2_relay(1)
    g2_relay(0)
    add_shard(strip[1], z)
    zl_relay(2)
    add_shard(l_all[left], left)
    add_shard(l_all[right], right)

    def g3(mode, k):
        g, to = group(mode, k)
        dst = (gram_r, gram_l)[mode].at[g_of[mode]]
        return remote(h.at[mode, k], dst, g3_s, g3_r, mode * NG + k, to, z)

    own_out = []

    def g2_to_g3(mode):
        g2_finish(mode)
        out = (gram_r, gram_l)[mode]
        for k in range(NG):
            g, to = group(mode, k)
            for q in range(NS):
                value = f[mode][source[mode, g * NS + q]]
                h[mode, k, q] = value
            if k:
                start(g3(mode, k))
            else:
                own_out.append(pltpu.make_async_copy(h.at[mode, 0], out.at[g], local_sem.at[14 + mode]))
                own_out[-1].start()

    g2_to_g3(1)
    g2_to_g3(0)
    zl_relay(3)
    add_shard(l_all[(z + 6) % NZ], (z + 6) % NZ)
    add_shard(l_all[(z + 2) % NZ], (z + 2) % NZ)
    add_shard(l_all[(z + 5) % NZ], (z + 5) % NZ)
    add_shard(l_all[(z + 3) % NZ], (z + 3) % NZ)
    zl_finish()
    add_shard(l_all[(z + 4) % NZ], (z + 4) % NZ)

    squares = jnp.zeros((8, TILE), F32)
    for a in range(NZ):
        rows = pre[a]
        squares = squares + jnp.sum((rows * rows).reshape(TILE // 8, 8, TILE), axis=0)
    ps[z, 1] = squares
    shares = [start(remote(ps.at[z], ps.at[z], ps_s, ps_r, k, d, (z + k) % NZ)) for k in (4, 3, 5, 2, 6, 1, 7)]
    for copy in shares:
        copy.wait_recv()

    def total(which):
        rows = jnp.sum(ps[:, which], axis=0)
        return jnp.sum(jnp.sum(rows, axis=0, keepdims=True), axis=1, keepdims=True)

    adam_sq = total(0).astype(BF16).astype(F32)
    scale = jnp.sqrt(adam_sq / (total(1) + norm_eps))
    for a in range(NZ):
        grafted[a * TILE:(a + 1) * TILE, :] = (pre[a] * scale).astype(BF16)
    own_out.append(pltpu.make_async_copy(grafted, graft, local_sem.at[16]))
    own_out[-1].start()

    for mode in (1, 0):
        for k in range(1, NG):
            g3(mode, k).wait_recv()
    for copy in own_out:
        copy.wait()
    flush()


def update(owners, graft, momentum, gram_l, gram_r, left_stats, right_stats, step, momentum_out, left_out, right_out):
    new = beta_one * momentum[0] + (1.0 - beta_one) * graft[...].astype(F32)
    momentum_out[0] = new
    step[0] = (-step_rate * new).astype(BF16)
    own = lax.axis_index("dp")
    count = jnp.int32(0)
    for b in range(NBLK):
        count += jnp.where(owners[b] == own, 1, 0)
    for q in range(NS):
        on = count > q
        for stats, gram, out in ((left_stats, gram_l, left_out), (right_stats, gram_r, right_out)):
            for c in range(NG):
                cols = slice(c * TILE, (c + 1) * TILE)
                term = jnp.where(on, gram[c, q].astype(F32), 0.0)
                out[0, q, :, cols] = beta_stat * stats[0, q, :, cols] + (1.0 - beta_stat) * term


def body(grads, momentum, second_moment, owners, left_stats, right_stats, left_roots, right_roots):
    vmem = lambda shape, dtype=BF16: pltpu.VMEM(shape, dtype)
    dma = lambda n: pltpu.SemaphoreType.DMA((n,))
    hbm = pl.BlockSpec(memory_space=pltpu.MemorySpace.HBM)
    tile = (TILE, TILE)
    graft, gram_l, gram_r = pl.pallas_call(
        kernel,
        name="shampoo",
        out_shape=(
            jax.ShapeDtypeStruct((BS, TILE), BF16),
            jax.ShapeDtypeStruct((NG, NS) + tile, BF16),
            jax.ShapeDtypeStruct((NG, NS) + tile, BF16),
        ),
        in_specs=[pl.BlockSpec(memory_space=pltpu.SMEM)] + [hbm] * 4,
        out_specs=[hbm] * 3,
        scratch_shapes=[
            vmem((NZ, BS, TILE)), vmem((BS, TILE), F32), vmem((2, NS, HALF, TILE)),
            vmem((NG * NS, PIECE, TILE)), vmem((NG * NS, PIECE, TILE)), vmem((2, 3 * NG, PIECE, TILE)),
            vmem((3 * NG, PIECE, TILE)), vmem((3 * NG, PIECE, TILE)), vmem((2, 2, NG // 2, PIECE, TILE)),
            vmem((2, NG, PIECE, TILE)), vmem((2, HALF, TILE)), vmem((3,) + tile),
            vmem((NZ, HALF, TILE)), vmem((2, NG) + tile), vmem((NT * NG,) + tile), vmem((NT * NG,) + tile), vmem((2, NG, NS) + tile),
            vmem((TILE, BS), F32), vmem((BS, TILE), F32), vmem((11,) + tile), vmem((TILE, BS)),
            vmem((NZ,) + tile, F32), vmem((NZ, 2, 8, TILE), F32), vmem((BS, TILE)),
            pltpu.SMEM((NBLK,), jnp.int32), pltpu.SMEM((2, NG * NS), jnp.int32),
            dma(17), dma(4), dma(4), dma(8 * CH), dma(8 * CH), dma(8 * CH), dma(8 * CH), dma(NZ), dma(NZ),
            dma(2 * NG), dma(2 * NG), dma(12), dma(12), dma(2 * NG), dma(2 * NG),
            dma(2 * NG), dma(2 * NG), dma(12), dma(12), dma(2 * NG), dma(2 * NG),
        ],
        compiler_params=pltpu.CompilerParams(collective_id=0, has_side_effects=True, vmem_limit_bytes=60 * 2**20),
    )(owners, grads, second_moment, left_roots, right_roots)

    steps = 2
    rows, wide = TILE // steps, BS // steps
    slab = pl.BlockSpec((1, wide, TILE), lambda i: (0, i, 0))
    stats = pl.BlockSpec((1, NS, rows, BS), lambda i: (0, 0, i, 0))
    gram = pl.BlockSpec((NG, NS, rows, TILE), lambda i: (0, 0, i, 0))
    return pl.pallas_call(
        update,
        name="update",
        grid=(steps,),
        out_shape=(
            jax.ShapeDtypeStruct((1, BS, TILE), BF16),
            jax.ShapeDtypeStruct((1, BS, TILE), F32),
            jax.ShapeDtypeStruct((1, NS, TILE, BS), F32),
            jax.ShapeDtypeStruct((1, NS, TILE, BS), F32),
        ),
        in_specs=[
            pl.BlockSpec(memory_space=pltpu.SMEM),
            pl.BlockSpec((wide, TILE), lambda i: (i, 0)),
            slab, gram, gram, stats, stats,
        ],
        out_specs=(slab, slab, stats, stats),
        compiler_params=pltpu.CompilerParams(vmem_limit_bytes=60 * 2**20),
    )(owners, graft, momentum, gram_l, gram_r, left_stats, right_stats)


def solution(mesh):
    return jax.shard_map(
        body,
        mesh=mesh,
        in_specs=(
            P("dp", None, "mp"),
            P("dp", None, "mp"),
            P("dp", None, "mp"),
            P(),
            P("dp", None, "mp", None),
            P("dp", None, "mp", None),
            P("dp", None, None, "mp"),
            P("dp", None, None, "mp"),
        ),
        out_specs=(
            P("dp", None, "mp"),
            P("dp", None, "mp"),
            P("dp", None, "mp", None),
            P("dp", None, "mp", None),
        ),
        check_vma=False,
    )
```

```python
import jax
import jax.numpy as jnp
from jax import lax
from jax.experimental import pallas as pl
from jax.experimental.pallas import tpu as pltpu
from jax.sharding import PartitionSpec as P

beta_one = 0.9
beta_adam = 0.99
beta_stat = 0.95
adam_eps = 1e-08
norm_eps = 1e-06
step_rate = 0.5

MESH = pl.DeviceIdType.MESH
NZ = 8
NG = 8
NT = 4
NBLK = 32
NS = 3
TILE = 128
BS = 1024
HALF = 5 * TILE
PIECE = HALF // NG
FAR = (4, 3, 5, 2, 6, 1, 7)
CH = 2
F32 = jnp.float32
BF16 = jnp.bfloat16


def dot(a, b, ca=1, cb=0):
    return lax.dot_general(a, b, (((ca,), (cb,)), ((), ())), preferred_element_type=F32)


def place(mode, i):
    if mode == 0:
        return i & 7, i >> 3
    return (i >> 3) * 2 + (i & 1), (i >> 1) & 3


def kernel(
    owners, grads, second, left_roots, right_roots,
    graft, gram_l, gram_r,
    gbuf, sec, rot, a_r, a_l, t_buf, b_r, b_l, via, c_buf, strip, cross,
    l_all, gram, f_r, f_l, h, lacc, acc, mext, gt, pre, ps, grafted,
    slot_of, source, local_sem, xr_s, xr_r, zg_s, zg_r, zl_s, zl_r, ps_s, ps_r, s1_s, s1_r, s2_s, s2_r, s3_s, s3_r, g1_s, g1_r, g2_s, g2_r, g3_s, g3_r,
):
    a, b, f = (a_r, a_l), (b_r, b_l), (f_r, f_l)
    d = lax.axis_index("dp")
    z = lax.axis_index("mp")
    core = d % 2
    x = (d // 2) % 4
    y = d // 8

    g_of = (x * 2 + core, y * 2 + core)
    t_of = (y, x)

    def dev(mode, g, t):
        if mode == 0:
            return t * 8 + g
        return (g // 2) * 8 + t * 2 + g % 2

    def group(mode, k):
        g = (g_of[mode] + k) % NG
        return g, dev(mode, g, t_of[mode])

    def other(mode, k):
        t = (t_of[mode] + k) % NT
        return t, dev(mode, g_of[mode], t)

    def remote(src, dst, ss, rs, i, to, zto):
        return pltpu.make_async_remote_copy(
            src_ref=src, dst_ref=dst, send_sem=ss.at[i], recv_sem=rs.at[i], device_id=(to, zto), device_id_type=MESH
        )

    sent = []

    def start(copy):
        copy.start()
        sent.append(copy)
        return copy

    barrier = pltpu.get_barrier_semaphore()
    partners = [(d, (z + k) % NZ) for k in (1, 7)]
    partners += [(group(0, k)[1], z) for k in range(1, NG)]
    for k in range(1, NT):
        for cc in range(2):
            partners.append((((y + k) % 4) * 8 + x * 2 + cc, z))
    for p in partners:
        pl.semaphore_signal(barrier, inc=1, device_id=p, device_id_type=MESH)
    def flush():
        for copy in sent:
            copy.wait_send()
        sent.clear()

    strips = []
    for mode in (1, 0):
        for j in range(5):
            row = pl.multiple_of(((z + j) % NZ) * TILE, TILE)
            copy = pltpu.make_async_copy(
                (right_roots, left_roots)[mode].at[0, :, pl.ds(row, TILE), :],
                rot.at[mode, :, pl.ds(j * TILE, TILE), :],
                local_sem.at[4 + 5 * mode + j],
            )
            copy.start()
            strips.append(copy)
    own_g = pltpu.make_async_copy(grads.at[0], gbuf.at[z], local_sem.at[0])
    own_g.start()
    own_sec = pltpu.make_async_copy(second.at[0], sec, local_sem.at[1])
    own_sec.start()

    pl.semaphore_wait(barrier, len(partners))

    right, left = (z + 1) % NZ, (z + NZ - 1) % NZ

    def ring(buf, rows, ss, rs, first):
        part = rows // CH

        def copy(direction, s, c):
            slot = (z + NZ - s) % NZ if direction == 0 else (z + s) % NZ
            i = (direction * 4 + s) * CH + c
            span = pl.ds(c * part, part)
            src = first(span) if s == 0 else buf.at[slot, span, :]
            to = right if direction == 0 else left
            return remote(src, buf.at[slot, span, :], ss, rs, i, d, to)

        def last_dir(c):
            return 0 if c < CH // 2 else 1

        def begin():
            for c in range(CH):
                start(copy(0, 0, c))
                start(copy(1, 0, c))

        def relay(s):
            for c in range(CH):
                for direction in range(2):
                    copy(direction, s - 1, c).wait_recv()
                    if s < 3 or last_dir(c) == direction:
                        start(copy(direction, s, c))

        def finish():
            for c in range(CH):
                copy(last_dir(c), 3, c).wait_recv()

        return begin, relay, finish

    zg_begin, zg_relay, zg_finish = ring(gbuf, BS, zg_s, zg_r, lambda span: grads.at[0, span, :])
    zg_begin()

    def find_slot(b, _):
        count = jnp.int32(0)
        for c in range(NBLK):
            count += jnp.where((owners[c] == owners[b]) & (c < b), 1, 0)
        slot_of[b] = jnp.minimum(count, NS - 1)
        return 0

    def find_blocks(i, _):
        for mode in range(2):
            o = dev(mode, i, t_of[mode])
            found = [jnp.int32(0)] * NS
            for b in range(NBLK):
                g, t = place(mode, b)
                mine = owners[b] == o
                for q in range(NS):
                    found[q] = jnp.where(mine & (slot_of[b] == q), t * NG + g, found[q])
            for q in range(NS):
                source[mode, i * NS + q] = found[q]
        return 0

    def piece(g):
        return pl.ds(pl.multiple_of(g * PIECE, 16), PIECE)

    def s1(mode, k):
        g, to = group(mode, k)
        dst = a[mode].at[pl.ds(g_of[mode] * NS, NS)]
        return remote(rot.at[mode, :, piece(g), :], dst, s1_s, s1_r, mode * NG + k, to, z)

    for copy in strips:
        copy.wait()
    own_pieces = []
    for mode in range(2):
        own_pieces.append(
            pltpu.make_async_copy(
                rot.at[mode, :, piece(g_of[mode]), :], a[mode].at[pl.ds(g_of[mode] * NS, NS)], local_sem.at[2 + mode]
            )
        )
        own_pieces[mode].start()
    for k in FAR:
        start(s1(1, k))
        start(s1(0, k))

    own_g.wait()
    own_sec.wait()

    def adam_rows(i, total):
        rows = pl.ds(pl.multiple_of(i * TILE, TILE), TILE)
        g = gbuf[z, rows, :].astype(F32)
        new = beta_adam * sec[rows, :] + (1.0 - beta_adam) * g * g
        direction = g / (jnp.sqrt(new) + adam_eps)
        return total + jnp.sum((direction * direction).reshape(TILE // 8, 8, TILE), axis=0)

    adam_part = lax.fori_loop(0, BS // TILE, adam_rows, jnp.zeros((8, TILE), F32))

    ps[z, 0] = adam_part
    lax.fori_loop(0, NBLK, find_slot, 0)
    gt[...] = gbuf[z].T
    own_rows = pl.ds(pl.multiple_of(z * TILE, TILE), TILE)

    def add_gram(shard, first=False):
        gram[0, shard] = dot(gt[...], gbuf[shard]).astype(BF16)
        term = dot(gbuf[shard, own_rows, :], gbuf[shard], 1, 1)
        lacc[...] = term if first else lacc[...] + term

    add_gram(z, True)
    zg_relay(1)

    def s2(mode, direction, kind):
        _, to = other(mode, 1 - 2 * direction + NT)
        half = (direction, 1 - direction, direction)[kind] * (NG // 2)
        src = (16, 8 * direction, 8 * direction)[kind] + half
        if kind == 0:
            dst = via.at[mode, direction]
        else:
            dst = b[mode].at[pl.ds(8 + 8 * direction + half, NG // 2)]
        i = (mode * 2 + direction) * 3 + kind
        return remote(t_buf.at[mode, pl.ds(src, NG // 2)], dst, s2_s, s2_r, i, to, z)

    def candidate(mode, g, t):
        b_id = dev(mode, g, t)
        g_owner, t_owner = place(mode, owners[b_id])
        return a[mode][g_owner * NS + slot_of[b_id]], t_owner

    def s1_to_s2(mode):
        own_pieces[mode].wait()
        for k in range(1, NG):
            s1(mode, k).wait_recv()
        opposite, _ = other(mode, 2)
        for direction in range(2):
            for g in range(4 * direction, 4 * direction + 4):
                t_buf[mode, 16 + g] = candidate(mode, g, opposite)[0]
            start(s2(mode, direction, 0))
        for direction in range(2):
            t, _ = other(mode, 1 - 2 * direction + NT)
            for g in range(4 - 4 * direction, 8 - 4 * direction):
                t_buf[mode, 8 * direction + g] = candidate(mode, g, t)[0]
            start(s2(mode, direction, 1))
        for g in range(NG):
            b[mode][g] = candidate(mode, g, t_of[mode])[0]

    def s2_merge(mode):
        for direction in range(2):
            s2(mode, direction, 0).wait_recv()
            k = 1 - 2 * direction
            t, _ = other(mode, k + NT)
            behind, _ = other(mode, NT - k)
            for i in range(4):
                g = 4 * direction + i
                value, t_owner = candidate(mode, g, t)
                t_buf[mode, 8 * direction + g] = jnp.where(t_owner == behind, via[mode, direction, i], value)
            start(s2(mode, direction, 2))

    s1_to_s2(1)
    s1_to_s2(0)
    lax.fori_loop(0, NG, find_blocks, 0)
    add_gram(left)
    add_gram(right)
    zg_relay(2)
    s2_merge(1)
    s2_merge(0)
    add_gram((z + 6) % NZ)
    add_gram((z + 2) % NZ)
    zg_relay(3)
    add_gram((z + 5) % NZ)
    add_gram((z + 3) % NZ)

    def s3(mode, k):
        g, to = group(mode, k)
        return remote(
            c_buf.at[mode, k], strip.at[mode, piece(g_of[mode]), :], s3_s, s3_r, mode * NG + k, to, z
        )

    def s2_to_s3(mode):
        for direction in range(2):
            for kind in (1, 2):
                s2(mode, direction, kind).wait_recv()
        for k in FAR + (0,):
            g, to = group(mode, k)
            steps = (place(mode, owners[to])[1] + NT - t_of[mode]) % NT
            side = jnp.where(steps == 3, 1, jnp.where(steps == 1, 2, jnp.where(g < 4, 1, 2)))
            value = b[mode][jnp.where(steps == 0, 0, side) * NG + g]
            if k:
                c_buf[mode, k] = value
                start(s3(mode, k))
            else:
                strip[mode, piece(g), :] = value

    def s3_done(mode):
        for k in range(1, NG):
            s3(mode, k).wait_recv()

    s2_to_s3(1)
    s2_to_s3(0)
    zg_finish()
    add_gram((z + 4) % NZ)

    def g1(mode, k):
        g, to = group(mode, k)
        dst = f[mode].at[t_of[mode] * NG + g_of[mode]]
        return remote(gram.at[mode, g], dst, g1_s, g1_r, mode * NG + k, to, z)

    for g in range(NG):
        gram[1, g] = lacc[:, g * TILE:(g + 1) * TILE].astype(BF16)
    for k in FAR + (0,):
        for mode in range(2):
            g, _ = group(mode, k)
            if k:
                start(g1(mode, k))
            else:
                f[mode][t_of[mode] * NG + g] = gram[mode, g]

    def xr(j):
        return remote(strip.at[0, pl.ds(j * TILE, TILE), :], cross.at[j - 1], xr_s, xr_r, j, d, (z + j) % NZ)

    s3_done(0)
    for j in (1, 2, 3):
        start(xr(j))

    s3_done(1)
    zl_begin, zl_relay, zl_finish = ring(l_all, HALF, zl_s, zl_r, lambda span: strip.at[1, span, :])
    zl_begin()

    def g2(mode, direction, kind):
        k = 1 - 2 * direction
        _, to = other(mode, k + NT)
        half = direction if kind != 1 else 1 - direction
        t = t_of[mode] if kind < 2 else (t_of[mode] + NT - k) % NT
        span = f[mode].at[pl.ds(t * NG + half * (NG // 2), NG // 2)]
        return remote(span, span, g2_s, g2_r, (mode * 2 + direction) * 3 + kind, to, z)

    def g2_begin(mode):
        for k in range(1, NG):
            g1(mode, k).wait_recv()
        for kind in range(2):
            for direction in range(2):
                start(g2(mode, direction, kind))

    def g2_relay(mode):
        for direction in range(2):
            g2(mode, direction, 0).wait_recv()
            start(g2(mode, direction, 2))

    def g2_finish(mode):
        for direction in range(2):
            for kind in (1, 2):
                g2(mode, direction, kind).wait_recv()

    g2_begin(1)
    g2_begin(0)

    acc[...] = dot(gbuf[z], strip[0, 0:TILE, :])
    for j in range(1, 5):
        acc[...] += dot(gbuf[(z + j) % NZ], strip[0, j * TILE:(j + 1) * TILE, :])
    for j in (1, 2, 3):
        xr(j).wait_recv()
        acc[...] += dot(gbuf[(z + NZ - j) % NZ], cross[j - 1], 1, 1)
    for j in range(11):
        mext[j] = acc[(j % NZ) * TILE:(j % NZ + 1) * TILE, :].astype(BF16)

    pre[...] = jnp.zeros((NZ, TILE, TILE), F32)

    def add_shard(shard, s):
        direct = dot(shard, mext[s])
        for j in range(5):
            row = (s + j) % NZ
            pre[row] += direct[j * TILE:(j + 1) * TILE, :]
        three = mext[pl.ds(s + 1, 3)].reshape(3 * TILE, TILE)
        pre[s] += dot(shard[TILE:4 * TILE, :], three, 0, 0)

    zl_relay(1)
    g2_relay(1)
    g2_relay(0)
    add_shard(strip[1], z)
    zl_relay(2)
    add_shard(l_all[left], left)
    add_shard(l_all[right], right)

    def g3(mode, k):
        g, to = group(mode, k)
        dst = (gram_r, gram_l)[mode].at[g_of[mode]]
        return remote(h.at[mode, k], dst, g3_s, g3_r, mode * NG + k, to, z)

    own_out = []

    def g2_to_g3(mode):
        g2_finish(mode)
        out = (gram_r, gram_l)[mode]
        for k in FAR + (0,):
            g, to = group(mode, k)
            for q in range(NS):
                value = f[mode][source[mode, g * NS + q]]
                h[mode, k, q] = value
            if k:
                start(g3(mode, k))
            else:
                own_out.append(pltpu.make_async_copy(h.at[mode, 0], out.at[g], local_sem.at[14 + mode]))
                own_out[-1].start()

    g2_to_g3(1)
    g2_to_g3(0)
    zl_relay(3)
    add_shard(l_all[(z + 6) % NZ], (z + 6) % NZ)
    add_shard(l_all[(z + 2) % NZ], (z + 2) % NZ)
    add_shard(l_all[(z + 5) % NZ], (z + 5) % NZ)
    add_shard(l_all[(z + 3) % NZ], (z + 3) % NZ)
    zl_finish()
    add_shard(l_all[(z + 4) % NZ], (z + 4) % NZ)

    squares = jnp.zeros((8, TILE), F32)
    for a in range(NZ):
        rows = pre[a]
        squares = squares + jnp.sum((rows * rows).reshape(TILE // 8, 8, TILE), axis=0)
    ps[z, 1] = squares
    shares = [start(remote(ps.at[z], ps.at[z], ps_s, ps_r, k, d, (z + k) % NZ)) for k in (4, 3, 5, 2, 6, 1, 7)]
    for copy in shares:
        copy.wait_recv()

    def total(which):
        rows = jnp.sum(ps[:, which], axis=0)
        return jnp.sum(jnp.sum(rows, axis=0, keepdims=True), axis=1, keepdims=True)

    adam_sq = total(0).astype(BF16).astype(F32)
    scale = jnp.sqrt(adam_sq / (total(1) + norm_eps))
    for a in range(NZ):
        grafted[a * TILE:(a + 1) * TILE, :] = (pre[a] * scale).astype(BF16)
    own_out.append(pltpu.make_async_copy(grafted, graft, local_sem.at[16]))
    own_out[-1].start()

    for mode in (1, 0):
        for k in range(1, NG):
            g3(mode, k).wait_recv()
    for copy in own_out:
        copy.wait()
    flush()


def update(owners, graft, momentum, gram_l, gram_r, left_stats, right_stats, step, momentum_out, left_out, right_out):
    new = beta_one * momentum[0] + (1.0 - beta_one) * graft[...].astype(F32)
    momentum_out[0] = new
    step[0] = (-step_rate * new).astype(BF16)
    own = lax.axis_index("dp")
    count = jnp.int32(0)
    for b in range(NBLK):
        count += jnp.where(owners[b] == own, 1, 0)
    for q in range(NS):
        on = count > q
        for stats, gram, out in ((left_stats, gram_l, left_out), (right_stats, gram_r, right_out)):
            for c in range(NG):
                cols = slice(c * TILE, (c + 1) * TILE)
                term = jnp.where(on, gram[c, q].astype(F32), 0.0)
                out[0, q, :, cols] = beta_stat * stats[0, q, :, cols] + (1.0 - beta_stat) * term


def body(grads, momentum, second_moment, owners, left_stats, right_stats, left_roots, right_roots):
    vmem = lambda shape, dtype=BF16: pltpu.VMEM(shape, dtype)
    dma = lambda n: pltpu.SemaphoreType.DMA((n,))
    hbm = pl.BlockSpec(memory_space=pltpu.MemorySpace.HBM)
    tile = (TILE, TILE)
    graft, gram_l, gram_r = pl.pallas_call(
        kernel,
        name="shampoo",
        out_shape=(
            jax.ShapeDtypeStruct((BS, TILE), BF16),
            jax.ShapeDtypeStruct((NG, NS) + tile, BF16),
            jax.ShapeDtypeStruct((NG, NS) + tile, BF16),
        ),
        in_specs=[pl.BlockSpec(memory_space=pltpu.SMEM)] + [hbm] * 4,
        out_specs=[hbm] * 3,
        scratch_shapes=[
            vmem((NZ, BS, TILE)), vmem((BS, TILE), F32), vmem((2, NS, HALF, TILE)),
            vmem((NG * NS, PIECE, TILE)), vmem((NG * NS, PIECE, TILE)), vmem((2, 3 * NG, PIECE, TILE)),
            vmem((3 * NG, PIECE, TILE)), vmem((3 * NG, PIECE, TILE)), vmem((2, 2, NG // 2, PIECE, TILE)),
            vmem((2, NG, PIECE, TILE)), vmem((2, HALF, TILE)), vmem((3,) + tile),
            vmem((NZ, HALF, TILE)), vmem((2, NG) + tile), vmem((NT * NG,) + tile), vmem((NT * NG,) + tile), vmem((2, NG, NS) + tile),
            vmem((TILE, BS), F32), vmem((BS, TILE), F32), vmem((11,) + tile), vmem((TILE, BS)),
            vmem((NZ,) + tile, F32), vmem((NZ, 2, 8, TILE), F32), vmem((BS, TILE)),
            pltpu.SMEM((NBLK,), jnp.int32), pltpu.SMEM((2, NG * NS), jnp.int32),
            dma(17), dma(4), dma(4), dma(8 * CH), dma(8 * CH), dma(8 * CH), dma(8 * CH), dma(NZ), dma(NZ),
            dma(2 * NG), dma(2 * NG), dma(12), dma(12), dma(2 * NG), dma(2 * NG),
            dma(2 * NG), dma(2 * NG), dma(12), dma(12), dma(2 * NG), dma(2 * NG),
        ],
        compiler_params=pltpu.CompilerParams(collective_id=0, has_side_effects=True, vmem_limit_bytes=60 * 2**20),
    )(owners, grads, second_moment, left_roots, right_roots)

    steps = 2
    rows, wide = TILE // steps, BS // steps
    slab = pl.BlockSpec((1, wide, TILE), lambda i: (0, i, 0))
    stats = pl.BlockSpec((1, NS, rows, BS), lambda i: (0, 0, i, 0))
    gram = pl.BlockSpec((NG, NS, rows, TILE), lambda i: (0, 0, i, 0))
    return pl.pallas_call(
        update,
        name="update",
        grid=(steps,),
        out_shape=(
            jax.ShapeDtypeStruct((1, BS, TILE), BF16),
            jax.ShapeDtypeStruct((1, BS, TILE), F32),
            jax.ShapeDtypeStruct((1, NS, TILE, BS), F32),
            jax.ShapeDtypeStruct((1, NS, TILE, BS), F32),
        ),
        in_specs=[
            pl.BlockSpec(memory_space=pltpu.SMEM),
            pl.BlockSpec((wide, TILE), lambda i: (i, 0)),
            slab, gram, gram, stats, stats,
        ],
        out_specs=(slab, slab, stats, stats),
        compiler_params=pltpu.CompilerParams(vmem_limit_bytes=60 * 2**20),
    )(owners, graft, momentum, gram_l, gram_r, left_stats, right_stats)


def solution(mesh):
    return jax.shard_map(
        body,
        mesh=mesh,
        in_specs=(
            P("dp", None, "mp"),
            P("dp", None, "mp"),
            P("dp", None, "mp"),
            P(),
            P("dp", None, "mp", None),
            P("dp", None, "mp", None),
            P("dp", None, None, "mp"),
            P("dp", None, None, "mp"),
        ),
        out_specs=(
            P("dp", None, "mp"),
            P("dp", None, "mp"),
            P("dp", None, "mp", None),
            P("dp", None, "mp", None),
        ),
        check_vma=False,
    )
```

```python
import jax
import jax.numpy as jnp
from jax import lax
from jax.experimental import pallas as pl
from jax.experimental.pallas import tpu as pltpu
from jax.sharding import PartitionSpec as P

beta_one = 0.9
beta_adam = 0.99
beta_stat = 0.95
adam_eps = 1e-08
norm_eps = 1e-06
step_rate = 0.5

MESH = pl.DeviceIdType.MESH
NZ = 8
NG = 8
NT = 4
NBLK = 32
NS = 3
TILE = 128
BS = 1024
HALF = 5 * TILE
PIECE = HALF // NG
FAR = (4, 3, 5, 2, 6, 1, 7)
CH = 2
F32 = jnp.float32
BF16 = jnp.bfloat16


def dot(a, b, ca=1, cb=0):
    return lax.dot_general(a, b, (((ca,), (cb,)), ((), ())), preferred_element_type=F32)


def place(mode, i):
    if mode == 0:
        return i & 7, i >> 3
    return (i >> 3) * 2 + (i & 1), (i >> 1) & 3


def kernel(
    owners, grads, second, left_roots, right_roots,
    graft, gram_l, gram_r,
    gbuf, sec, rot, a_r, a_l, t_buf, b_r, b_l, via, c_buf, strip, cross,
    l_all, gram, f_r, f_l, h, lacc, acc, mext, gt, pre, ps, grafted,
    slot_of, source, local_sem, xr_s, xr_r, zg_s, zg_r, zl_s, zl_r, ps_s, ps_r, s1_s, s1_r, s2_s, s2_r, s3_s, s3_r, g1_s, g1_r, g2_s, g2_r, g3_s, g3_r,
):
    a, b, f = (a_r, a_l), (b_r, b_l), (f_r, f_l)
    d = lax.axis_index("dp")
    z = lax.axis_index("mp")
    core = d % 2
    x = (d // 2) % 4
    y = d // 8

    g_of = (x * 2 + core, y * 2 + core)
    t_of = (y, x)

    def dev(mode, g, t):
        if mode == 0:
            return t * 8 + g
        return (g // 2) * 8 + t * 2 + g % 2

    def group(mode, k):
        g = (g_of[mode] + k) % NG
        return g, dev(mode, g, t_of[mode])

    def other(mode, k):
        t = (t_of[mode] + k) % NT
        return t, dev(mode, g_of[mode], t)

    def remote(src, dst, ss, rs, i, to, zto):
        return pltpu.make_async_remote_copy(
            src_ref=src, dst_ref=dst, send_sem=ss.at[i], recv_sem=rs.at[i], device_id=(to, zto), device_id_type=MESH
        )

    sent = []

    def start(copy):
        copy.start()
        sent.append(copy)
        return copy

    barrier = pltpu.get_barrier_semaphore()
    partners = [(d, (z + k) % NZ) for k in (1, 7)]
    partners += [(group(0, k)[1], z) for k in range(1, NG)]
    for k in range(1, NT):
        for cc in range(2):
            partners.append((((y + k) % 4) * 8 + x * 2 + cc, z))
    for p in partners:
        pl.semaphore_signal(barrier, inc=1, device_id=p, device_id_type=MESH)
    def flush():
        for copy in sent:
            copy.wait_send()
        sent.clear()

    strips = []
    for mode in (1, 0):
        for j in range(5):
            row = pl.multiple_of(((z + j) % NZ) * TILE, TILE)
            copy = pltpu.make_async_copy(
                (right_roots, left_roots)[mode].at[0, :, pl.ds(row, TILE), :],
                rot.at[mode, :, pl.ds(j * TILE, TILE), :],
                local_sem.at[4 + 5 * mode + j],
            )
            copy.start()
            strips.append(copy)
    own_g = pltpu.make_async_copy(grads.at[0], gbuf.at[z], local_sem.at[0])
    own_g.start()
    own_sec = pltpu.make_async_copy(second.at[0], sec, local_sem.at[1])
    own_sec.start()

    pl.semaphore_wait(barrier, len(partners))

    right, left = (z + 1) % NZ, (z + NZ - 1) % NZ

    def ring(buf, rows, ss, rs, first):
        part = rows // CH

        def copy(direction, s, c):
            slot = (z + NZ - s) % NZ if direction == 0 else (z + s) % NZ
            i = (direction * 4 + s) * CH + c
            span = pl.ds(c * part, part)
            src = first(span) if s == 0 else buf.at[slot, span, :]
            to = right if direction == 0 else left
            return remote(src, buf.at[slot, span, :], ss, rs, i, d, to)

        def last_dir(c):
            return 0 if c < CH // 2 else 1

        def begin():
            for c in range(CH):
                start(copy(0, 0, c))
                start(copy(1, 0, c))

        def relay(s):
            for c in range(CH):
                for direction in range(2):
                    copy(direction, s - 1, c).wait_recv()
                    if s < 3 or last_dir(c) == direction:
                        start(copy(direction, s, c))

        def finish():
            for c in range(CH):
                copy(last_dir(c), 3, c).wait_recv()

        return begin, relay, finish

    zg_begin, zg_relay, zg_finish = ring(gbuf, BS, zg_s, zg_r, lambda span: grads.at[0, span, :])
    zg_begin()

    def find_slot(b, _):
        count = jnp.int32(0)
        for c in range(NBLK):
            count += jnp.where((owners[c] == owners[b]) & (c < b), 1, 0)
        slot_of[b] = jnp.minimum(count, NS - 1)
        return 0

    def find_blocks(i, _):
        for mode in range(2):
            o = dev(mode, i, t_of[mode])
            found = [jnp.int32(0)] * NS
            for b in range(NBLK):
                g, t = place(mode, b)
                mine = owners[b] == o
                for q in range(NS):
                    found[q] = jnp.where(mine & (slot_of[b] == q), t * NG + g, found[q])
            for q in range(NS):
                source[mode, i * NS + q] = found[q]
        return 0

    def piece(g):
        return pl.ds(pl.multiple_of(g * PIECE, 16), PIECE)

    def s1(mode, k):
        g, to = group(mode, k)
        dst = a[mode].at[pl.ds(g_of[mode] * NS, NS)]
        return remote(rot.at[mode, :, piece(g), :], dst, s1_s, s1_r, mode * NG + k, to, z)

    for copy in strips:
        copy.wait()
    own_pieces = []
    for mode in range(2):
        own_pieces.append(
            pltpu.make_async_copy(
                rot.at[mode, :, piece(g_of[mode]), :], a[mode].at[pl.ds(g_of[mode] * NS, NS)], local_sem.at[2 + mode]
            )
        )
        own_pieces[mode].start()
    for k in FAR:
        start(s1(1, k))
        start(s1(0, k))

    own_g.wait()
    own_sec.wait()

    def adam_rows(i, total):
        rows = pl.ds(pl.multiple_of(i * TILE, TILE), TILE)
        g = gbuf[z, rows, :].astype(F32)
        new = beta_adam * sec[rows, :] + (1.0 - beta_adam) * g * g
        direction = g / (jnp.sqrt(new) + adam_eps)
        return total + jnp.sum((direction * direction).reshape(TILE // 8, 8, TILE), axis=0)

    adam_part = lax.fori_loop(0, BS // TILE, adam_rows, jnp.zeros((8, TILE), F32))

    ps[z, 0] = adam_part
    lax.fori_loop(0, NBLK, find_slot, 0)
    gt[...] = gbuf[z].T
    own_rows = pl.ds(pl.multiple_of(z * TILE, TILE), TILE)

    def add_gram(shard, first=False):
        gram[0, shard] = dot(gt[...], gbuf[shard]).astype(BF16)
        term = dot(gbuf[shard, own_rows, :], gbuf[shard], 1, 1)
        lacc[...] = term if first else lacc[...] + term

    add_gram(z, True)
    zg_relay(1)

    def s2(mode, direction, kind):
        _, to = other(mode, 1 - 2 * direction + NT)
        half = (direction, 1 - direction, direction)[kind] * (NG // 2)
        src = (16, 8 * direction, 8 * direction)[kind] + half
        if kind == 0:
            dst = via.at[mode, direction]
        else:
            dst = b[mode].at[pl.ds(8 + 8 * direction + half, NG // 2)]
        i = (mode * 2 + direction) * 3 + kind
        return remote(t_buf.at[mode, pl.ds(src, NG // 2)], dst, s2_s, s2_r, i, to, z)

    def candidate(mode, g, t):
        b_id = dev(mode, g, t)
        g_owner, t_owner = place(mode, owners[b_id])
        return a[mode][g_owner * NS + slot_of[b_id]], t_owner

    def s1_to_s2(mode):
        own_pieces[mode].wait()
        for k in range(1, NG):
            s1(mode, k).wait_recv()
        opposite, _ = other(mode, 2)
        for direction in range(2):
            for g in range(4 * direction, 4 * direction + 4):
                t_buf[mode, 16 + g] = candidate(mode, g, opposite)[0]
            start(s2(mode, direction, 0))
        for direction in range(2):
            t, _ = other(mode, 1 - 2 * direction + NT)
            for g in range(4 - 4 * direction, 8 - 4 * direction):
                t_buf[mode, 8 * direction + g] = candidate(mode, g, t)[0]
            start(s2(mode, direction, 1))
        for g in range(NG):
            b[mode][g] = candidate(mode, g, t_of[mode])[0]

    def s2_merge(mode):
        for direction in range(2):
            s2(mode, direction, 0).wait_recv()
            k = 1 - 2 * direction
            t, _ = other(mode, k + NT)
            behind, _ = other(mode, NT - k)
            for i in range(4):
                g = 4 * direction + i
                value, t_owner = candidate(mode, g, t)
                t_buf[mode, 8 * direction + g] = jnp.where(t_owner == behind, via[mode, direction, i], value)
            start(s2(mode, direction, 2))

    s1_to_s2(1)
    s1_to_s2(0)
    add_gram(left)
    add_gram(right)
    zg_relay(2)
    s2_merge(1)
    s2_merge(0)
    add_gram((z + 6) % NZ)
    add_gram((z + 2) % NZ)
    zg_relay(3)
    lax.fori_loop(0, NG, find_blocks, 0)
    add_gram((z + 5) % NZ)
    add_gram((z + 3) % NZ)

    def s3(mode, k):
        g, to = group(mode, k)
        return remote(
            c_buf.at[mode, k], strip.at[mode, piece(g_of[mode]), :], s3_s, s3_r, mode * NG + k, to, z
        )

    def s2_to_s3(mode):
        for direction in range(2):
            for kind in (1, 2):
                s2(mode, direction, kind).wait_recv()
        for k in FAR + (0,):
            g, to = group(mode, k)
            steps = (place(mode, owners[to])[1] + NT - t_of[mode]) % NT
            side = jnp.where(steps == 3, 1, jnp.where(steps == 1, 2, jnp.where(g < 4, 1, 2)))
            value = b[mode][jnp.where(steps == 0, 0, side) * NG + g]
            if k:
                c_buf[mode, k] = value
                start(s3(mode, k))
            else:
                strip[mode, piece(g), :] = value

    def s3_done(mode):
        for k in range(1, NG):
            s3(mode, k).wait_recv()

    s2_to_s3(1)
    s2_to_s3(0)
    zg_finish()
    add_gram((z + 4) % NZ)

    def g1(mode, k):
        g, to = group(mode, k)
        dst = f[mode].at[t_of[mode] * NG + g_of[mode]]
        return remote(gram.at[mode, g], dst, g1_s, g1_r, mode * NG + k, to, z)

    for g in range(NG):
        gram[1, g] = lacc[:, g * TILE:(g + 1) * TILE].astype(BF16)
    for k in FAR + (0,):
        for mode in range(2):
            g, _ = group(mode, k)
            if k:
                start(g1(mode, k))
            else:
                f[mode][t_of[mode] * NG + g] = gram[mode, g]

    def xr(j):
        return remote(strip.at[0, pl.ds(j * TILE, TILE), :], cross.at[j - 1], xr_s, xr_r, j, d, (z + j) % NZ)

    s3_done(0)
    for j in (1, 2, 3):
        start(xr(j))

    s3_done(1)
    zl_begin, zl_relay, zl_finish = ring(l_all, HALF, zl_s, zl_r, lambda span: strip.at[1, span, :])
    zl_begin()

    def g2(mode, direction, kind):
        k = 1 - 2 * direction
        _, to = other(mode, k + NT)
        half = direction if kind != 1 else 1 - direction
        t = t_of[mode] if kind < 2 else (t_of[mode] + NT - k) % NT
        span = f[mode].at[pl.ds(t * NG + half * (NG // 2), NG // 2)]
        return remote(span, span, g2_s, g2_r, (mode * 2 + direction) * 3 + kind, to, z)

    def g2_begin(mode):
        for k in range(1, NG):
            g1(mode, k).wait_recv()
        for kind in range(2):
            for direction in range(2):
                start(g2(mode, direction, kind))

    def g2_relay(mode):
        for direction in range(2):
            g2(mode, direction, 0).wait_recv()
            start(g2(mode, direction, 2))

    def g2_finish(mode):
        for direction in range(2):
            for kind in (1, 2):
                g2(mode, direction, kind).wait_recv()

    g2_begin(1)
    g2_begin(0)

    acc[...] = dot(gbuf[z], strip[0, 0:TILE, :])
    for j in range(1, 5):
        acc[...] += dot(gbuf[(z + j) % NZ], strip[0, j * TILE:(j + 1) * TILE, :])
    for j in (1, 2, 3):
        xr(j).wait_recv()
        acc[...] += dot(gbuf[(z + NZ - j) % NZ], cross[j - 1], 1, 1)
    for j in range(11):
        mext[j] = acc[(j % NZ) * TILE:(j % NZ + 1) * TILE, :].astype(BF16)

    pre[...] = jnp.zeros((NZ, TILE, TILE), F32)

    def add_shard(shard, s):
        direct = dot(shard, mext[s])
        for j in range(5):
            row = (s + j) % NZ
            pre[row] += direct[j * TILE:(j + 1) * TILE, :]
        three = mext[pl.ds(s + 1, 3)].reshape(3 * TILE, TILE)
        pre[s] += dot(shard[TILE:4 * TILE, :], three, 0, 0)

    zl_relay(1)
    g2_relay(1)
    g2_relay(0)
    add_shard(strip[1], z)
    zl_relay(2)
    add_shard(l_all[left], left)
    add_shard(l_all[right], right)

    def g3(mode, k):
        g, to = group(mode, k)
        dst = (gram_r, gram_l)[mode].at[g_of[mode]]
        return remote(h.at[mode, k], dst, g3_s, g3_r, mode * NG + k, to, z)

    own_out = []

    def g2_to_g3(mode):
        g2_finish(mode)
        out = (gram_r, gram_l)[mode]
        for k in FAR + (0,):
            g, to = group(mode, k)
            for q in range(NS):
                value = f[mode][source[mode, g * NS + q]]
                h[mode, k, q] = value
            if k:
                start(g3(mode, k))
            else:
                own_out.append(pltpu.make_async_copy(h.at[mode, 0], out.at[g], local_sem.at[14 + mode]))
                own_out[-1].start()

    g2_to_g3(1)
    g2_to_g3(0)
    zl_relay(3)
    add_shard(l_all[(z + 6) % NZ], (z + 6) % NZ)
    add_shard(l_all[(z + 2) % NZ], (z + 2) % NZ)
    add_shard(l_all[(z + 5) % NZ], (z + 5) % NZ)
    add_shard(l_all[(z + 3) % NZ], (z + 3) % NZ)
    zl_finish()
    add_shard(l_all[(z + 4) % NZ], (z + 4) % NZ)

    squares = jnp.zeros((8, TILE), F32)
    for a in range(NZ):
        rows = pre[a]
        squares = squares + jnp.sum((rows * rows).reshape(TILE // 8, 8, TILE), axis=0)
    ps[z, 1] = squares
    shares = [start(remote(ps.at[z], ps.at[z], ps_s, ps_r, k, d, (z + k) % NZ)) for k in (4, 3, 5, 2, 6, 1, 7)]
    for copy in shares:
        copy.wait_recv()

    def total(which):
        rows = jnp.sum(ps[:, which], axis=0)
        return jnp.sum(jnp.sum(rows, axis=0, keepdims=True), axis=1, keepdims=True)

    adam_sq = total(0).astype(BF16).astype(F32)
    scale = jnp.sqrt(adam_sq / (total(1) + norm_eps))
    for a in range(NZ):
        grafted[a * TILE:(a + 1) * TILE, :] = (pre[a] * scale).astype(BF16)
    own_out.append(pltpu.make_async_copy(grafted, graft, local_sem.at[16]))
    own_out[-1].start()

    for mode in (1, 0):
        for k in range(1, NG):
            g3(mode, k).wait_recv()
    for copy in own_out:
        copy.wait()
    flush()


def update(owners, graft, momentum, gram_l, gram_r, left_stats, right_stats, step, momentum_out, left_out, right_out):
    new = beta_one * momentum[0] + (1.0 - beta_one) * graft[...].astype(F32)
    momentum_out[0] = new
    step[0] = (-step_rate * new).astype(BF16)
    own = lax.axis_index("dp")
    count = jnp.int32(0)
    for b in range(NBLK):
        count += jnp.where(owners[b] == own, 1, 0)
    for q in range(NS):
        on = count > q
        for stats, gram, out in ((left_stats, gram_l, left_out), (right_stats, gram_r, right_out)):
            for c in range(NG):
                cols = slice(c * TILE, (c + 1) * TILE)
                term = jnp.where(on, gram[c, q].astype(F32), 0.0)
                out[0, q, :, cols] = beta_stat * stats[0, q, :, cols] + (1.0 - beta_stat) * term


def body(grads, momentum, second_moment, owners, left_stats, right_stats, left_roots, right_roots):
    vmem = lambda shape, dtype=BF16: pltpu.VMEM(shape, dtype)
    dma = lambda n: pltpu.SemaphoreType.DMA((n,))
    hbm = pl.BlockSpec(memory_space=pltpu.MemorySpace.HBM)
    tile = (TILE, TILE)
    graft, gram_l, gram_r = pl.pallas_call(
        kernel,
        name="shampoo",
        out_shape=(
            jax.ShapeDtypeStruct((BS, TILE), BF16),
            jax.ShapeDtypeStruct((NG, NS) + tile, BF16),
            jax.ShapeDtypeStruct((NG, NS) + tile, BF16),
        ),
        in_specs=[pl.BlockSpec(memory_space=pltpu.SMEM)] + [hbm] * 4,
        out_specs=[hbm] * 3,
        scratch_shapes=[
            vmem((NZ, BS, TILE)), vmem((BS, TILE), F32), vmem((2, NS, HALF, TILE)),
            vmem((NG * NS, PIECE, TILE)), vmem((NG * NS, PIECE, TILE)), vmem((2, 3 * NG, PIECE, TILE)),
            vmem((3 * NG, PIECE, TILE)), vmem((3 * NG, PIECE, TILE)), vmem((2, 2, NG // 2, PIECE, TILE)),
            vmem((2, NG, PIECE, TILE)), vmem((2, HALF, TILE)), vmem((3,) + tile),
            vmem((NZ, HALF, TILE)), vmem((2, NG) + tile), vmem((NT * NG,) + tile), vmem((NT * NG,) + tile), vmem((2, NG, NS) + tile),
            vmem((TILE, BS), F32), vmem((BS, TILE), F32), vmem((11,) + tile), vmem((TILE, BS)),
            vmem((NZ,) + tile, F32), vmem((NZ, 2, 8, TILE), F32), vmem((BS, TILE)),
            pltpu.SMEM((NBLK,), jnp.int32), pltpu.SMEM((2, NG * NS), jnp.int32),
            dma(17), dma(4), dma(4), dma(8 * CH), dma(8 * CH), dma(8 * CH), dma(8 * CH), dma(NZ), dma(NZ),
            dma(2 * NG), dma(2 * NG), dma(12), dma(12), dma(2 * NG), dma(2 * NG),
            dma(2 * NG), dma(2 * NG), dma(12), dma(12), dma(2 * NG), dma(2 * NG),
        ],
        compiler_params=pltpu.CompilerParams(collective_id=0, has_side_effects=True, vmem_limit_bytes=60 * 2**20),
    )(owners, grads, second_moment, left_roots, right_roots)

    steps = 2
    rows, wide = TILE // steps, BS // steps
    slab = pl.BlockSpec((1, wide, TILE), lambda i: (0, i, 0))
    stats = pl.BlockSpec((1, NS, rows, BS), lambda i: (0, 0, i, 0))
    gram = pl.BlockSpec((NG, NS, rows, TILE), lambda i: (0, 0, i, 0))
    return pl.pallas_call(
        update,
        name="update",
        grid=(steps,),
        out_shape=(
            jax.ShapeDtypeStruct((1, BS, TILE), BF16),
            jax.ShapeDtypeStruct((1, BS, TILE), F32),
            jax.ShapeDtypeStruct((1, NS, TILE, BS), F32),
            jax.ShapeDtypeStruct((1, NS, TILE, BS), F32),
        ),
        in_specs=[
            pl.BlockSpec(memory_space=pltpu.SMEM),
            pl.BlockSpec((wide, TILE), lambda i: (i, 0)),
            slab, gram, gram, stats, stats,
        ],
        out_specs=(slab, slab, stats, stats),
        compiler_params=pltpu.CompilerParams(vmem_limit_bytes=60 * 2**20),
    )(owners, graft, momentum, gram_l, gram_r, left_stats, right_stats)


def solution(mesh):
    return jax.shard_map(
        body,
        mesh=mesh,
        in_specs=(
            P("dp", None, "mp"),
            P("dp", None, "mp"),
            P("dp", None, "mp"),
            P(),
            P("dp", None, "mp", None),
            P("dp", None, "mp", None),
            P("dp", None, None, "mp"),
            P("dp", None, None, "mp"),
        ),
        out_specs=(
            P("dp", None, "mp"),
            P("dp", None, "mp"),
            P("dp", None, "mp", None),
            P("dp", None, "mp", None),
        ),
        check_vma=False,
    )
```
